128 devices in a mesh: dp: 4 (over x_hi, core), blk: 4 (over z), tensor: 8 (over y, x_lo).
Axes of the slice: x: 4 (x_hi: 2, x_lo: 2; x = x_hi * 2 + x_lo), y: 4, z: 4, core: 2. Of those that a mesh axis runs over, the one named last changes fastest.
Arguments:
- hidden_in: bfloat16 [2048, 12, 1024], P(('blk', 'tensor'), 'dp'), may hold values from -6 to 6
- out_grad: bfloat16 [2048, 12, 1024], P(('blk', 'tensor'), 'dp'), may hold values from -6 to 6
- norm_scales: float32 [2, 1024], replicated, may hold values from 0.1 to 1.9
- norm_shifts: float32 [2, 1024], replicated, may hold values from -3 to 3
- w_qkv: bfloat16 [3, 1024, 1024], P(None, None, 'tensor'), may hold values from -0.25 to 0.25
- w_out: bfloat16 [1024, 1024], P('tensor'), may hold values from -0.75 to 0.75
- w_gate_up: bfloat16 [2, 1024, 4096], P(None, None, 'tensor'), may hold values from -0.1875 to 0.1875
- w_down: bfloat16 [4096, 1024], P('tensor'), may hold values from -0.125 to 0.125
- lengths: int32 [12], P('dp'), may hold values from 256 to 2048, as said below
Outputs:
- result: bfloat16 [2048, 12, 1024], P(('blk', 'tensor'), 'dp')
- grad_input: bfloat16 [2048, 12, 1024], P(('blk', 'tensor'), 'dp')
- grad_qkv: float32 [3, 1024, 1024], P(None, None, 'tensor')
- grad_out_proj: float32 [1024, 1024], P('tensor')
- grad_gate_up: float32 [2, 1024, 4096], P(None, None, 'tensor')
- grad_down: float32 [4096, 1024], P('tensor')
- grad_scales: float32 [2, 1024], replicated
- grad_shifts: float32 [2, 1024], replicated
The draws below stay inside these ranges and needn't reach their ends.
Inputs may be any that keep to these rules, and one draw needn't show every extreme that they name: `lengths`: each group of 3 consecutive windows (one index of dp) holds at least one window of length 2048; tokens at or past a window's length are padding, whose keys are masked.
All inputs are finite; a program needn't handle non-finite values.
Results may differ from the reference program's by a relative error of at most 0.03.
Values may be sent and summed in bfloat16 or wider, within the bound.
No kernel may reach another device: no remote copies, remote signals or barrier semaphores. Data moves between devices by JAX's collectives and lax.ppermute only.
A program may use at most 192 MiB of HBM per device.

```python
import math
from functools import partial
import jax
import jax.numpy as jnp
from jax import lax

D = 1024
HD = 64
FF = 4096
SEQ = 2048
WIN = 3
WINDOWS = 12


def draw_lengths(key, part):
    key = jax.random.fold_in(key, 11)
    key_lengths, key_picked = jax.random.split(key)
    drawn = jax.random.randint(key_lengths, (WINDOWS,), SEQ // 8, SEQ + 1)
    picked = jax.random.randint(key_picked, (WINDOWS // WIN,), 0, WIN)
    is_full = jnp.arange(WINDOWS) % WIN == jnp.repeat(picked, WIN)
    return jnp.where(is_full, SEQ, drawn).astype(jnp.int32)


def levels(key, extent, pieces, low, top_value):
    def one(position, parts):
        steps = jax.random.uniform(jax.random.fold_in(jax.random.fold_in(key, 6), position), (parts,), jnp.float32, low / len(pieces), top_value / len(pieces))
        return jnp.repeat(jnp.exp(steps), extent[position] // parts).reshape((-1,) + (1,) * (len(extent) - position - 1))

    factor_of = one(*pieces[0])
    for cut in pieces[1:]:
        factor_of = factor_of * one(*cut)
    return factor_of


def gaussian(key, extent, deviation, most, cuts=(), held_as=jnp.bfloat16):
    entries = jax.random.normal(key, extent, jnp.float32) * deviation
    if len(cuts) > 0:
        entries = levels(key, extent, cuts, -0.22, 0.18) * entries
    return jnp.clip(entries, min=-most, max=most).astype(held_as)


def setup_inputs(seed: int = 0) -> dict:
    streams_of = jax.random.split(jax.random.key(seed), 10)
    return {
        "hidden_in": gaussian(streams_of[0], (SEQ, WINDOWS, D), 1.0, 6.0, ((0, 32), (1, 4))),
        "out_grad": gaussian(streams_of[1], (SEQ, WINDOWS, D), 1.0, 6.0, ((0, 32), (1, 4))),
        "norm_scales": jnp.clip(1.0 + 0.18 * jax.random.normal(streams_of[2], (2, D), jnp.float32), 0.1, 1.9),
        "norm_shifts": gaussian(streams_of[3], (2, D), 0.5, 3.0, (), jnp.float32),
        "w_qkv": gaussian(streams_of[4], (3, D, D), (D // 2) ** -0.5, 0.25, ((2, 8),)),
        "w_out": gaussian(streams_of[5], (D, D), (D // 16) ** -0.5, 0.75, ((0, 8),)),
        "w_gate_up": gaussian(streams_of[6], (2, D, FF), D ** -0.5, 0.1875, ((2, 8),)),
        "w_down": gaussian(streams_of[7], (FF, D), (FF // 2) ** -0.5, 0.125, ((0, 8),)),
        "lengths": draw_lengths(jax.random.fold_in(streams_of[9], 71), 0),
    }


HIGHEST_PRECISION = lax.Precision.HIGHEST
EPSILON = 1e-05
MASKED = -1000000000.0

@jax.custom_vjp
def low(v):
    return lax.optimization_barrier(v.astype(jnp.bfloat16)).astype(jnp.float32)

@jax.custom_vjp
def low_back(v):
    return v

def low_keep(v):
    return (low(v), None)

def low_pass(kept, grad):
    return (grad,)

def back_keep(v):
    return (v, None)

def back_low(kept, grad):
    return (low(grad),)
low.defvjp(low_keep, low_pass)
low_back.defvjp(back_keep, back_low)

def norm_rows(values, gain_row, offset_row):
    row_mean = lax.optimization_barrier(jnp.mean(values, axis=-1, keepdims=True))
    centred = values - row_mean
    row_var = lax.optimization_barrier(jnp.mean(centred * centred, axis=-1, keepdims=True))
    return centred * lax.rsqrt(row_var + EPSILON) * gain_row + offset_row

def rope_tables(length):
    inverse = 10000.0 ** (-(jnp.arange(HD // 2, dtype=jnp.float32) * 2.0) / HD)
    angles = jnp.arange(length, dtype=jnp.float32)[:, None] * inverse[None, :]
    angles = jnp.concatenate([angles, angles], axis=-1)
    return (jnp.cos(angles), jnp.sin(angles))

def rotate_fwd(values, cosine, sine_table):
    half_width = values.shape[-1] // 2
    turned = jnp.concatenate([-values[..., half_width:], values[..., :half_width]], axis=-1)
    return values * cosine + turned * sine_table

def attend_head(head_items, lengths):
    queries, key_rows, value_rows = head_items
    scores = jnp.einsum('sgc,tgc->gst', queries, key_rows, precision=HIGHEST_PRECISION) * 0.125
    scores = low_back(scores)
    visible = jnp.arange(key_rows.shape[0], dtype=jnp.int32)[None, :] < lengths[:, None]
    scores = jnp.where(visible[:, None, :], scores, MASKED)
    row_top = lax.optimization_barrier(jnp.max(scores, axis=-1, keepdims=True))
    log_total = row_top + jnp.log(lax.optimization_barrier(jnp.sum(jnp.exp(scores - row_top), axis=-1, keepdims=True)))
    weights = low(jnp.exp(scores - log_total))
    return jnp.einsum('gst,tgc->sgc', weights, value_rows, precision=HIGHEST_PRECISION)

def block_forward(inputs, lengths, norm_scales, norm_shifts, w_qkv, w_out, w_gate_up, w_down):
    seq_rows, group_size, width = inputs.shape
    head_count = w_qkv.shape[2] // HD
    normed_one = low(norm_rows(inputs, norm_scales[0], norm_shifts[0]))
    projected = jnp.einsum('sgd,kde->ksge', normed_one, w_qkv, precision=HIGHEST_PRECISION)
    cosine, sine_table = rope_tables(seq_rows)
    cosine = cosine[:, None, None, :]
    sine_table = sine_table[:, None, None, :]
    query_pre = low_back(projected[0]).reshape(seq_rows, group_size, head_count, HD)
    key_pre = low_back(projected[1]).reshape(seq_rows, group_size, head_count, HD)
    queries = low(rotate_fwd(query_pre, cosine, sine_table))
    key_rows = low(rotate_fwd(key_pre, cosine, sine_table))
    value_rows = low_back(low(projected[2])).reshape(seq_rows, group_size, head_count, HD)
    head_fn = jax.checkpoint(partial(attend_head, lengths=lengths))
    attended = lax.map(head_fn, (jnp.moveaxis(queries, 2, 0), jnp.moveaxis(key_rows, 2, 0), jnp.moveaxis(value_rows, 2, 0)))
    attended = jnp.moveaxis(attended, 0, 2).reshape(seq_rows, group_size, head_count * HD)
    attended = low_back(low(attended))
    middle = inputs + low_back(jnp.einsum('sgd,de->sge', attended, w_out, precision=HIGHEST_PRECISION))
    normed_two = low(norm_rows(middle, norm_scales[1], norm_shifts[1]))
    gate_up = jnp.einsum('sgd,kdf->ksgf', normed_two, w_gate_up, precision=HIGHEST_PRECISION)
    hidden = low(jax.nn.silu(low_back(gate_up[0])) * low_back(gate_up[1]))
    return middle + low_back(jnp.einsum('sgf,fd->sgd', hidden, w_down, precision=HIGHEST_PRECISION))

def reference(hidden_in, out_grad, norm_scales, norm_shifts, w_qkv, w_out, w_gate_up, w_down, lengths):
    group_size = math.gcd(WINDOWS, max(1, 4096 // SEQ))
    group_count = WINDOWS // group_size
    params = tuple((item.astype(jnp.float32) for item in (norm_scales, norm_shifts, w_qkv, w_out, w_gate_up, w_down)))
    inputs = hidden_in.astype(jnp.float32).reshape(SEQ, group_count, group_size, D).transpose(1, 0, 2, 3)
    cotangent = out_grad.astype(jnp.float32).reshape(SEQ, group_count, group_size, D).transpose(1, 0, 2, 3)
    group_lengths = lengths.reshape(group_count, group_size).astype(jnp.int32)

    def group_step(running, items):
        group_in, group_cot, group_len = items

        def forward(values, *weights):
            return block_forward(values, group_len, *weights)
        outputs, pullback = jax.vjp(forward, group_in, *params)
        grads = pullback(group_cot)
        running = tuple((accum + grad_piece for accum, grad_piece in zip(running, grads[1:])))
        return (running, (outputs.astype(jnp.bfloat16), grads[0].astype(jnp.bfloat16)))
    zeros = tuple((jnp.zeros_like(item) for item in params))
    totals, (outputs, input_grads) = lax.scan(group_step, zeros, (inputs, cotangent, group_lengths))
    result = outputs.transpose(1, 0, 2, 3).reshape(SEQ, WINDOWS, D)
    grad_input = input_grads.transpose(1, 0, 2, 3).reshape(SEQ, WINDOWS, D)
    return (result, grad_input, totals[2], totals[3], totals[4], totals[5], totals[0], totals[1])
```

```python
import jax
import jax.numpy as jnp
from jax import lax
from jax.experimental import pallas as pl
from jax.experimental.pallas import tpu as pltpu
from jax.sharding import PartitionSpec as P

HD = 64
EPSILON = 1e-05
MASKED = -1000000000.0
F32 = jnp.float32
BF16 = jnp.bfloat16
VMEM_LIMIT = 48 * 1024 * 1024


def send_y(values, step):
    pairs = [(i, ((i // 2 + step) % 4) * 2 + i % 2) for i in range(8)]
    return lax.ppermute(values, "tensor", pairs)


def send_pair(values):
    return lax.ppermute(values, "tensor", [(i, i ^ 1) for i in range(8)])


def send_z(values, step):
    return lax.ppermute(values, "blk", [(i, (i + step) % 4) for i in range(4)])


def send_core(values):
    return lax.ppermute(values, "dp", [(i, i ^ 1) for i in range(4)])


def send_far(values):
    return lax.ppermute(values, "dp", [(i, i ^ 2) for i in range(4)])


def send_x(values, steps):
    pairs = []
    for d in range(4):
        for t in range(8):
            core = d % 2
            x = ((d // 2) * 2 + t % 2 + steps[core]) % 4
            pairs.append((d * 8 + t, ((x // 2) * 2 + core) * 8 + (t // 2) * 2 + x % 2))
    return lax.ppermute(values, ("dp", "tensor"), pairs)


def gather_y(values):
    return [values] + [send_y(values, -r) for r in (1, 2, 3)]


def scatter_y(total):
    rows = total.shape[0] // 4
    parts = [lax.slice_in_dim(total, r * rows, (r + 1) * rows, axis=0) for r in range(4)]
    out = parts[0].astype(F32)
    for r in (1, 2, 3):
        out = out + send_y(parts[r], r).astype(F32)
    return out


def norm_parts(values):
    mean = jnp.mean(values, axis=-1, keepdims=True)
    centred = values - mean
    inverse = lax.rsqrt(jnp.mean(centred * centred, axis=-1, keepdims=True) + EPSILON)
    return centred * inverse, inverse


def norm_back(normed, inverse, gain, cotangent):
    e = cotangent * gain
    grad = (
        e
        - jnp.mean(e, axis=-1, keepdims=True)
        - normed * jnp.mean(e * normed, axis=-1, keepdims=True)
    ) * inverse
    return grad, jnp.sum(cotangent * normed, axis=0), jnp.sum(cotangent, axis=0)


def dot(a, b, ca, cb):
    return lax.dot_general(a, b, (((ca,), (cb,)), ((), ())), preferred_element_type=F32)


def load_keys(own, pair, bias):
    keys = jnp.concatenate([r[:HD, :] for r in own + pair], axis=1)
    values = jnp.concatenate([r[HD:, :] for r in own + pair], axis=1)
    row = lax.broadcasted_iota(jnp.int32, (16, keys.shape[1]), 0)
    extra = jnp.where(row == 0, bias[...], 0.0).astype(BF16)
    return keys, values, jnp.concatenate([keys, extra], axis=0)


def with_one(queries):
    row = lax.broadcasted_iota(jnp.int32, (16, queries.shape[1]), 0)
    return jnp.concatenate([queries, jnp.where(row == 0, 1.0, 0.0).astype(BF16)], axis=0)


def attend_kernel(*refs):
    q, own, pair, bias = refs[0:4], refs[4:8], refs[8:12], refs[12]
    out, wide, lse = refs[13:17], refs[17], refs[18]
    _, values, keys_bias = load_keys(own, pair, bias)
    keys_rows = keys_bias.T
    for i in range(4):
        scores = dot(keys_rows, with_one(q[i][...]), 1, 0)
        top = jnp.max(scores, axis=0, keepdims=True)
        weights = jnp.exp(scores - top)
        total = jnp.sum(weights, axis=0, keepdims=True)
        attended = dot(values, weights.astype(BF16), 1, 0) * (1.0 / total)
        wide[i] = attended
        out[i][...] = attended.astype(BF16)
        lse[i] = top + jnp.log(total)


def attend_back_kernel(*refs):
    q, own, pair, bias = refs[0:4], refs[4:8], refs[8:12], refs[12]
    dob, wide, lse = refs[13:17], refs[17], refs[18]
    dq, d_own, d_pair = refs[19:23], refs[23:27], refs[27:31]
    keys, values, keys_bias = load_keys(own, pair, bias)
    keys_rows = keys_bias.T
    values_rows = values.T
    dk = jnp.zeros((keys.shape[1], HD), F32)
    dv = jnp.zeros((keys.shape[1], HD), F32)
    for i in range(4):
        queries, grad = q[i][...], dob[i][...]
        scores = dot(keys_rows, with_one(queries), 1, 0)
        weights = jnp.exp(scores - lse[i])
        delta = jnp.sum(grad.astype(F32) * wide[i], axis=0, keepdims=True)
        grad_weights = dot(values_rows, grad, 1, 0)
        grad_scores = (weights * (grad_weights - delta)).astype(BF16)
        dq[i][...] = (dot(keys, grad_scores, 1, 0) * 0.125).astype(BF16)
        dk = dk + dot(grad_scores, queries, 1, 1)
        dv = dv + dot(weights.astype(BF16), grad, 1, 1)
    dkv = jnp.concatenate([dk, dv], axis=1).T
    width = q[0].shape[1]
    for i, ref in enumerate(d_own + d_pair):
        ref[...] = dkv[:, i * width : (i + 1) * width].astype(BF16)


def attend(q, own, pair, bias):
    width = q[0].shape[1]
    piece = jax.ShapeDtypeStruct((HD, width), BF16)
    out = pl.pallas_call(
        attend_kernel,
        out_shape=[piece] * 4
        + [jax.ShapeDtypeStruct((4, HD, width), F32), jax.ShapeDtypeStruct((4, 1, width), F32)],
        compiler_params=pltpu.CompilerParams(vmem_limit_bytes=VMEM_LIMIT),
        cost_estimate=pl.CostEstimate(
            flops=4 * 4 * width * 8 * width * HD, bytes_accessed=3_000_000, transcendentals=0
        ),
        name="attend",
    )(*q, *own, *pair, bias)
    return list(out[:4]), out[4], out[5]


def attend_back(q, own, pair, bias, dob, wide, lse):
    width = q[0].shape[1]
    piece = jax.ShapeDtypeStruct((HD, width), BF16)
    double = jax.ShapeDtypeStruct((2 * HD, width), BF16)
    out = pl.pallas_call(
        attend_back_kernel,
        out_shape=[piece] * 4 + [double] * 8,
        compiler_params=pltpu.CompilerParams(vmem_limit_bytes=VMEM_LIMIT),
        cost_estimate=pl.CostEstimate(
            flops=10 * 4 * width * 8 * width * HD, bytes_accessed=3_000_000, transcendentals=0
        ),
        name="attend_back",
    )(*q, *own, *pair, bias, *dob, wide, lse)
    return list(out[:4]), list(out[4:8]), list(out[8:12])


def pick(values, index, size=1, axis=0):
    return lax.dynamic_slice_in_dim(values, index, size, axis)


def sum_over_copies(grads, z):
    out = []
    for grad in grads:
        rows = grad.shape[0] // 4
        part = pick(grad, z * rows, rows).astype(F32)
        for r in (1, 2, 3):
            part = part + send_z(pick(grad, ((z + r) % 4) * rows, rows), r).astype(F32)
        low = part.astype(BF16)
        low = (low.astype(F32) + send_far(low).astype(F32)).astype(BF16)
        ring = [low] + [send_z(low, -r) for r in (1, 2, 3)]
        ring = jnp.concatenate(ring + ring, axis=0)
        out.append(pick(ring, ((4 - z) % 4) * rows, 4 * rows))
    return out


def shards(hidden_in, out_grad, norm_scales, norm_shifts, w_qkv, w_out, w_gate_up, w_down, lengths):
    rows, windows, width = hidden_in.shape
    tensor = lax.axis_index("tensor")
    y, xl = tensor // 2, tensor % 2
    z = lax.axis_index("blk")
    core = lax.axis_index("dp") % 2
    tokens = 4 * rows
    ff = w_down.shape[0]
    half = ff // 2

    x_own = [hidden_in[:, w, :] for w in range(windows)]
    dy_own = [out_grad[:, w, :] for w in range(windows)]
    x_all = [jnp.concatenate(gather_y(v), axis=0) for v in x_own]

    heads_own = jnp.concatenate(
        [
            w_qkv.reshape(3, width, 2, HD).transpose(2, 0, 3, 1).reshape(2, 3 * HD, width),
            w_out.reshape(2, HD, width),
        ],
        axis=1,
    )
    heads_recv = send_x(pick(heads_own, core), (-1, 1))
    heads_four = jnp.concatenate([heads_own, heads_recv, send_core(heads_recv)], axis=0)
    gate_up_recv = send_x(pick(w_gate_up, core * half, half, 2), (-1, 1))
    down_recv = send_x(pick(w_down, core * half, half, 0), (-1, 1))
    w_gu = jnp.concatenate([w_gate_up, gate_up_recv, send_core(gate_up_recv)], axis=2)
    w_gu = jnp.concatenate([w_gu[0], w_gu[1]], axis=1)
    w_d = jnp.concatenate([w_down, down_recv, send_core(down_recv)], axis=0)

    heads_rel = []
    for r in range(4):
        head = (z + r) % 4
        place = jnp.where(head // 2 == xl, head % 2, 2 + ((head % 2) ^ core))
        heads_rel.append(pick(heads_four, place))
    heads_rel = jnp.concatenate(heads_rel, axis=0)
    w_in = heads_rel[:, : 3 * HD].reshape(12 * HD, width)
    w_back = heads_rel[:, 3 * HD :].reshape(4 * HD, width)

    dy_all = [jnp.concatenate(gather_y(v), axis=0) for v in dy_own]

    lane = jnp.arange(tokens, dtype=jnp.int32)
    within = ((y + lane // rows) % 4) * (2 * rows) + lane % rows
    inverse = 10000.0 ** (-(jnp.arange(HD // 2, dtype=F32) * 2.0) / HD)
    angles = inverse[:, None] * (z * (8 * rows) + within + xl * rows).astype(F32)[None, :]
    cosine, sine = jnp.cos(angles), jnp.sin(angles)
    key_places = jnp.concatenate(
        [
            ((z - r) % 4) * (8 * rows) + within + side * rows
            for side in (xl, 1 - xl)
            for r in range(4)
        ]
    )
    bias = [
        jnp.where(key_places < lengths[w], 0.0, MASKED).astype(F32)[None, :] for w in range(windows)
    ]

    saved = []
    for w in range(windows):
        normed, _ = norm_parts(x_all[w].astype(F32))
        h1 = (normed * norm_scales[0] + norm_shifts[0]).astype(BF16)
        proj = dot(w_in, h1, 1, 1).reshape(4, 3, 2, HD // 2, tokens)
        first, second = proj[:, :2, 0], proj[:, :2, 1]
        turned = jnp.stack([first * cosine - second * sine, second * cosine + first * sine], axis=2)
        q_send = (turned[:, 0] * 0.125).astype(BF16).reshape(4, HD, tokens)
        kv_send = jnp.stack([turned[:, 1], proj[:, 2]], axis=1).astype(BF16)
        kv_send = kv_send.reshape(4, 2 * HD, tokens)
        q = [q_send[0]] + [send_z(q_send[r], r) for r in (1, 2, 3)]
        own = [kv_send[0]] + [send_z(kv_send[r], r) for r in (1, 2, 3)]
        pair = [send_pair(v) for v in own]
        out, wide, lse = attend(q, own, pair, bias[w])
        ob = jnp.concatenate([out[0]] + [send_z(out[r], -r) for r in (1, 2, 3)], axis=0)
        attn = scatter_y(dot(ob, w_back, 0, 0).astype(BF16))
        middle = x_own[w].astype(F32) + attn
        saved.append((h1, q, own, pair, wide, lse, ob, middle))

    ffn = []
    for w in range(windows):
        middle = saved[w][7]
        normed, inv = norm_parts(middle)
        h2 = jnp.concatenate(
            gather_y((normed * norm_scales[1] + norm_shifts[1]).astype(BF16)), axis=0
        )
        gate_up = dot(h2, w_gu, 1, 0)
        gate, up = gate_up[:, : 2 * ff], gate_up[:, 2 * ff :]
        sig = jax.nn.sigmoid(gate)
        act = gate * sig
        hid = (act * up).astype(BF16)
        dh = dot(dy_all[w], w_d, 1, 1)
        d_gate = (dh * up * (sig * (1.0 + gate * (1.0 - sig)))).astype(BF16)
        d_up = (dh * act).astype(BF16)
        d_gu = jnp.concatenate([d_gate, d_up], axis=1)
        dh2 = scatter_y(dot(d_gu, w_gu, 1, 1).astype(BF16))
        y_out = scatter_y(dot(hid, w_d, 1, 0).astype(BF16))
        result = (middle + y_out).astype(BF16)
        back, g_scale, g_shift = norm_back(normed, inv, norm_scales[1], dh2)
        dx2 = dy_own[w].astype(F32) + back
        ffn.append((h2, hid, d_gu, result, dx2, g_scale, g_shift))

    g_d = sum(dot(ffn[w][1], dy_all[w], 0, 0) for w in range(windows)).astype(BF16)
    g_gu = sum(dot(ffn[w][0], ffn[w][2], 0, 0) for w in range(windows)).astype(BF16)
    g_g, g_u = g_gu[:, : 2 * ff], g_gu[:, 2 * ff :]

    def own_half(values, which, axis):
        return pick(lax.slice_in_dim(values, 0, ff, axis=axis), which * half, half, axis)

    def far_half(values, which, axis):
        return lax.slice_in_dim(values, ff + which * half, ff + (which + 1) * half, axis=axis)

    keep_gu = [jnp.concatenate([own_half(g, core, 1) for g in (g_g, g_u)], axis=1)]
    keep_gu.append(jnp.concatenate([far_half(g, 0, 1) for g in (g_g, g_u)], axis=1))
    give_gu = [jnp.concatenate([own_half(g, 1 - core, 1) for g in (g_g, g_u)], axis=1)]
    give_gu.append(jnp.concatenate([far_half(g, 1, 1) for g in (g_g, g_u)], axis=1))
    keep_d = [own_half(g_d, core, 0), far_half(g_d, 0, 0)]
    give_d = [own_half(g_d, 1 - core, 0), far_half(g_d, 1, 0)]

    def add(a, b):
        return (a.astype(F32) + b.astype(F32)).astype(BF16)

    def fold(keep, give):
        own, far = (add(k, send_core(g)) for k, g in zip(keep, give))
        return add(own, send_x(far, (-1, 1)))

    sum_gu, sum_d = sum_over_copies([fold(keep_gu, give_gu), fold(keep_d, give_d)], z)

    def both(mine, axis):
        other = send_core(mine)
        low = jnp.where(core == 0, mine, other).astype(F32)
        high = jnp.where(core == 0, other, mine).astype(F32)
        return jnp.concatenate([low, high], axis=axis)

    grad_gate_up = jnp.stack([both(sum_gu[:, :half], 1), both(sum_gu[:, half:], 1)])
    grad_down = both(sum_d, 0)

    g_in, g_back = 0.0, 0.0
    grads_in, scales, shifts = [], [], []
    for w in range(windows):
        h1, q, own, pair, wide, lse, ob, _ = saved[w]
        dx2 = ffn[w][4]
        da = jnp.concatenate(gather_y(dx2.astype(BF16)), axis=0)
        g_back = g_back + dot(ob, da, 1, 0)
        dob_send = dot(w_back, da, 1, 1).astype(BF16).reshape(4, HD, tokens)
        dob = [dob_send[0]] + [send_z(dob_send[r], r) for r in (1, 2, 3)]
        dq, d_own, d_pair = attend_back(q, own, pair, bias[w], dob, wide, lse)
        d_kv = [add(a, send_pair(b)) for a, b in zip(d_own, d_pair)]
        dq = [dq[0]] + [send_z(dq[r], -r) for r in (1, 2, 3)]
        d_kv = [d_kv[0]] + [send_z(d_kv[r], -r) for r in (1, 2, 3)]
        pieces = []
        for r in range(4):
            for grad in (dq[r], d_kv[r][:HD]):
                first, second = grad[: HD // 2].astype(F32), grad[HD // 2 :].astype(F32)
                pieces.append((first * cosine + second * sine).astype(BF16))
                pieces.append((second * cosine - first * sine).astype(BF16))
            pieces.append(d_kv[r][HD:])
        d_proj = jnp.concatenate(pieces, axis=0)
        g_in = g_in + dot(d_proj, h1, 1, 0)
        dh1 = scatter_y(dot(d_proj, w_in, 0, 0).astype(BF16))
        normed, inv = norm_parts(x_own[w].astype(F32))
        back, g_scale, g_shift = norm_back(normed, inv, norm_scales[0], dh1)
        grads_in.append((dx2 + back).astype(BF16))
        scales.append(g_scale)
        shifts.append(g_shift)

    g_heads = jnp.concatenate(
        [g_in.reshape(4, 3 * HD, width), g_back.reshape(4, HD, width)], axis=1
    ).astype(BF16)

    def head_at(head):
        return pick(g_heads, (head - z) % 4)[0]

    keep = [head_at(2 * xl + core), head_at(2 * (1 - xl) + core)]
    give = [head_at(2 * xl + 1 - core), head_at(2 * (1 - xl) + 1 - core)]
    (sum_heads,) = sum_over_copies([fold(keep, give)], z)
    heads = both(sum_heads[None], 0)
    grad_qkv = heads[:, : 3 * HD].reshape(2, 3, HD, width).transpose(1, 3, 0, 2)
    grad_qkv = grad_qkv.reshape(3, width, 2 * HD)
    grad_out = heads[:, 3 * HD :].reshape(2 * HD, width)

    small = jnp.stack([sum(scales), sum(f[5] for f in ffn), sum(shifts), sum(f[6] for f in ffn)])
    small = small + send_core(small)
    small = small + sum(send_y(small, r) for r in (1, 2, 3))
    small = small + sum(send_x(small, (r, r)) for r in (1, 2, 3))
    small = small + sum(send_z(small, r) for r in (1, 2, 3))

    return (
        jnp.stack([f[3] for f in ffn], axis=1),
        jnp.stack(grads_in, axis=1),
        grad_qkv,
        grad_out,
        grad_gate_up,
        grad_down,
        small[:2],
        small[2:],
    )


def solution(mesh):
    placed = (
        P(("blk", "tensor"), "dp", None),
        P(("blk", "tensor"), "dp", None),
        P(),
        P(),
        P(None, None, "tensor"),
        P("tensor", None),
        P(None, None, "tensor"),
        P("tensor", None),
        P("dp"),
    )
    return jax.shard_map(
        shards,
        mesh=mesh,
        in_specs=placed,
        out_specs=(
            P(("blk", "tensor"), "dp", None),
            P(("blk", "tensor"), "dp", None),
            P(None, None, "tensor"),
            P("tensor", None),
            P(None, None, "tensor"),
            P("tensor", None),
            P(),
            P(),
        ),
        check_vma=False,
    )
```

```python
import functools
import math

import jax
import jax.numpy as jnp
from jax import lax
from jax.experimental import pallas as pl
from jax.experimental.pallas import tpu as pltpu
from jax.sharding import PartitionSpec as P

HD = 64
EPSILON = 1e-05
MASKED = -1000000000.0
F32 = jnp.float32
BF16 = jnp.bfloat16
MIB = 1024 * 1024


def send_y(values, step):
    pairs = [(i, ((i // 2 + step) % 4) * 2 + i % 2) for i in range(8)]
    return lax.ppermute(values, "tensor", pairs)


def send_pair(values):
    return lax.ppermute(values, "tensor", [(i, i ^ 1) for i in range(8)])


def send_z(values, step):
    return lax.ppermute(values, "blk", [(i, (i + step) % 4) for i in range(4)])


def send_core(values):
    return lax.ppermute(values, "dp", [(i, i ^ 1) for i in range(4)])


def send_far(values):
    return lax.ppermute(values, "dp", [(i, i ^ 2) for i in range(4)])


def send_x(values, steps):
    pairs = []
    for d in range(4):
        for t in range(8):
            core = d % 2
            x = ((d // 2) * 2 + t % 2 + steps[core]) % 4
            pairs.append((d * 8 + t, ((x // 2) * 2 + core) * 8 + (t // 2) * 2 + x % 2))
    return lax.ppermute(values, ("dp", "tensor"), pairs)


def gather_y(values):
    return [values] + [send_y(values, -r) for r in (1, 2, 3)]


def scatter_y(parts):
    return [parts[0]] + [send_y(parts[r], r) for r in (1, 2, 3)]


def gather_z(parts):
    return [parts[0]] + [send_z(parts[r], r) for r in (1, 2, 3)]


def scatter_z(parts):
    return [parts[0]] + [send_z(parts[r], -r) for r in (1, 2, 3)]


def norm_parts(values):
    mean = jnp.mean(values, axis=-1, keepdims=True)
    centred = values - mean
    inverse = lax.rsqrt(jnp.mean(centred * centred, axis=-1, keepdims=True) + EPSILON)
    return centred * inverse, inverse


def norm_back(normed, inverse, gain, cotangent):
    e = cotangent * gain
    grad = (
        e
        - jnp.mean(e, axis=-1, keepdims=True)
        - normed * jnp.mean(e * normed, axis=-1, keepdims=True)
    ) * inverse
    return grad, jnp.sum(cotangent * normed, axis=0), jnp.sum(cotangent, axis=0)


def dot(a, b, ca, cb):
    return lax.dot_general(a, b, (((ca,), (cb,)), ((), ())), preferred_element_type=F32)


def rows_of(refs):
    return jnp.concatenate([r[...] for r in refs], axis=0)


def put_rows(refs, values):
    rows = refs[0].shape[0]
    for i, ref in enumerate(refs):
        ref[...] = values[i * rows : (i + 1) * rows].astype(ref.dtype)


def call(kernel, name, inputs, outs, flops, after=(), mib=8):
    count = len(inputs)

    def body(*refs):
        kernel(refs[:count], refs[count + len(after) :])

    moved = sum(v.size * v.dtype.itemsize for v in inputs)
    moved += sum(math.prod(shape) * jnp.dtype(dtype).itemsize for shape, dtype in outs)
    return pl.pallas_call(
        body,
        in_specs=[
            pl.BlockSpec(memory_space=pltpu.SMEM if v.dtype == jnp.int32 else pltpu.VMEM)
            for v in inputs
        ]
        + [pl.BlockSpec(memory_space=pl.ANY)] * len(after),
        out_specs=[pl.BlockSpec(memory_space=pltpu.VMEM)] * len(outs),
        out_shape=[jax.ShapeDtypeStruct(shape, dtype) for shape, dtype in outs],
        compiler_params=pltpu.CompilerParams(vmem_limit_bytes=mib * MIB),
        cost_estimate=pl.CostEstimate(flops=flops, bytes_accessed=moved, transcendentals=0),
        name=name,
    )(*inputs, *after)


def project_kernel(ins, outs):
    normed, _ = norm_parts(rows_of(ins[:4]).astype(F32))
    w_in, gain, offset, cosine, sine = ins[4:9]
    outs[4][...] = normed.astype(BF16)
    h1 = (normed * gain[...] + offset[...]).astype(BF16)
    proj = dot(w_in[...], h1, 1, 1)
    c, s = cosine[...], sine[...]
    half = HD // 2
    for r in range(4):
        for part in range(3):
            at = (3 * r + part) * HD
            first, second = proj[at : at + half], proj[at + half : at + HD]
            if part < 2:
                first, second = first * c - second * s, second * c + first * s
            if part == 0:
                first, second = first * 0.125, second * 0.125
            outs[r][part * HD : part * HD + half, :] = first.astype(BF16)
            outs[r][part * HD + half : (part + 1) * HD, :] = second.astype(BF16)


def out_kernel(ins, outs):
    ob = rows_of(ins[:4])
    outs[4][...] = ob
    put_rows(outs[:4], dot(ob.T, ins[4][...], 1, 0))


def middle_kernel(ins, outs):
    middle = sum(r[...].astype(F32) for r in ins[:5])
    normed, _ = norm_parts(middle)
    outs[0][...] = middle
    outs[1][...] = (normed * ins[5][...] + ins[6][...]).astype(BF16)


def middle_back_kernel(ins, outs):
    dh2 = sum(r[...].astype(F32) for r in ins[:4])
    normed, inv = norm_parts(ins[4][...])
    back, g_scale, g_shift = norm_back(normed, inv, ins[6][...], dh2)
    dx2 = ins[5][...].astype(F32) + back
    outs[0][...] = dx2
    outs[1][...] = dx2.astype(BF16)
    outs[2][...] = jnp.concatenate([g_scale[None], g_shift[None]], axis=0)


def out_back_kernel(ins, outs):
    da = rows_of(ins[:4])
    outs[4][...] = da
    put_rows(outs[:4], dot(ins[4][...], da, 1, 1))


def merge_kernel(ins, outs):
    for r in range(4):
        outs[r][:HD, :] = ins[r][:HD, :]
        total = ins[r][HD:, :].astype(F32) + ins[4][r].astype(F32)
        outs[r][HD:, :] = total.astype(BF16)


def project_back_kernel(ins, outs):
    w_in, cosine, sine = ins[4:7]
    c, s = cosine[...], sine[...]
    half = HD // 2
    pieces = []
    for r in range(4):
        for part in range(2):
            first = ins[r][part * HD : part * HD + half, :].astype(F32)
            second = ins[r][part * HD + half : (part + 1) * HD, :].astype(F32)
            pieces.append((first * c + second * s).astype(BF16))
            pieces.append((second * c - first * s).astype(BF16))
        pieces.append(ins[r][2 * HD :, :])
    d_proj = jnp.concatenate(pieces, axis=0)
    outs[4][...] = d_proj
    put_rows(outs[:4], dot(d_proj.T, w_in[...], 1, 0))


def input_back_kernel(ins, outs):
    dh1 = sum(r[...].astype(F32) for r in ins[:4])
    normed, inv = norm_parts(ins[4][...].astype(F32))
    back, _, _ = norm_back(normed, inv, ins[6][...], dh1)
    outs[0][...] = (ins[5][...] + back).astype(BF16)


def heads_part_kernel(ins, outs):
    total, sums = 0.0, 0.0
    for d_proj, normed in zip(ins[0::2], ins[1::2]):
        total = total + dot(d_proj[...], normed[...], 1, 0)
        sums = sums + jnp.sum(d_proj[...].astype(F32), axis=1, keepdims=True)
    outs[0][...] = total
    outs[1][...] = jnp.broadcast_to(sums, outs[1].shape)


def heads_kernel(ins, outs):
    d_proj, normed, part, part_sum, back, w_in, gain, offset, slots = ins[:9]
    total = part[...] + dot(d_proj[...], normed[...], 1, 0)
    sums = part_sum[:, :1] + jnp.sum(d_proj[...].astype(F32), axis=1, keepdims=True)
    g_in = (total * gain[...] + sums * offset[...]).astype(BF16)
    wide = w_in[...].astype(F32)
    second = sum(r[...] for r in ins[9:])
    small = [
        jnp.sum(wide * total, axis=0, keepdims=True),
        second[:1],
        jnp.sum(wide * sums, axis=0, keepdims=True),
        second[1:],
    ]
    row = lax.broadcasted_iota(jnp.int32, (16, g_in.shape[1]), 0)
    small = [jnp.where(row == 0, v, 0.0).astype(BF16) for v in small]

    def put(out, slot, r):
        for chunk in range(4):
            if chunk < 3:
                rows = g_in[3 * HD * r + HD * chunk : 3 * HD * r + HD * (chunk + 1)]
            else:
                rows = back[HD * r : HD * (r + 1)].astype(BF16)
            out[slot, chunk, :HD] = rows
            out[slot, chunk, HD:] = small[chunk]

    for r in range(4):
        slot = slots[r]

        @pl.when(slot < 2)
        def _(slot=slot, r=r):
            put(outs[0], slot, r)

        @pl.when(slot >= 2)
        def _(slot=slot, r=r):
            put(outs[1], slot - 2, r)


def heads_core_kernel(ins, outs):
    for i in range(2):
        outs[i][...] = (ins[0][i].astype(F32) + ins[1][i].astype(F32)).astype(BF16)


def heads_pair_kernel(ins, outs):
    for r in range(4):
        chunk = lax.rem(ins[2][0] + r, 4)
        outs[r][...] = (ins[0][chunk].astype(F32) + ins[1][chunk].astype(F32)).astype(BF16)


def sum_kernel(ins, outs):
    outs[0][...] = sum(r[...].astype(F32) for r in ins).astype(outs[0].dtype)


def heads_ring_kernel(ins, outs):
    for r in range(4):
        chunk = lax.rem(ins[4][0] + r, 4)
        outs[0][chunk] = ins[r][...]
    for r in range(4):
        outs[1][lax.rem(ins[4][0] + r, 4)] = ins[r][HD : HD + 1].astype(F32)


def out_grad_kernel(ins, outs):
    total = 0.0
    for ob, da in zip(ins[0::2], ins[1::2]):
        total = total + dot(ob[...], da[...], 1, 0)
    outs[0][...] = total


def by_core(core, mine, other):
    low = jnp.where(core == 0, mine, other).astype(F32)
    high = jnp.where(core == 0, other, mine).astype(F32)
    return low, high


def units_final_kernel(ins, outs):
    low, high = by_core(ins[2][0], ins[0][...], ins[1][...])
    half = low.shape[0] // 3
    for side, values in enumerate((low, high)):
        for part in range(2):
            outs[0][part, :, side * half : (side + 1) * half] = values[
                part * half : (part + 1) * half
            ].T
        outs[1][side * half : (side + 1) * half] = values[2 * half :]


def heads_final_kernel(ins, outs):
    low, high = by_core(ins[2][0], ins[0][:, :HD], ins[1][:, :HD])
    for part in range(3):
        outs[0][part] = jnp.concatenate([low[part], high[part]], axis=0).T
    outs[1][...] = jnp.concatenate([low[3], high[3]], axis=0)


def stack_kernel(ins, outs):
    for r in range(4):
        outs[r][...] = jnp.concatenate([v[r] for v in ins], axis=0)


def result_kernel(ins, outs):
    total = sum(r[...].astype(F32) for r in ins[:4])
    rows = ins[4].shape[0]
    for w, middle in enumerate(ins[4:]):
        outs[0][w] = (middle[...] + total[w * rows : (w + 1) * rows]).astype(BF16)


def ffn_kernel(window, ins, outs):
    h2_in, dy_in, own, recv, other, y = ins[0:4], *ins[4:9]
    dh2_out, y_out, hid_out, d_gu_out, h2_out, dy_out = outs[0:4], *outs[4:9]
    rows, block = h2_in[0].shape[0], own.shape[2]
    h2_all = rows_of(h2_in)
    dy_all = jnp.concatenate([dy_in[lax.rem(y[0] + r, 4), window] for r in range(4)], axis=0)
    h2_out[...] = h2_all
    dy_out[...] = dy_all
    acc_dh2, acc_y = 0.0, 0.0
    for i, (w_gate, w_up, w_down) in enumerate(
        [[own[j, part] for part in range(3)] for j in range(2)]
        + [[ref[part] for part in range(3)] for ref in (recv, other)]
    ):
        gate = dot(h2_all, w_gate, 1, 1)
        up = dot(h2_all, w_up, 1, 1)
        dh = dot(dy_all, w_down, 1, 1)
        sig = 1.0 / (1.0 + jnp.exp(-gate))
        act = gate * sig
        hid = (act * up).astype(BF16)
        d_gate = (dh * up * (sig + act * (1.0 - sig))).astype(BF16)
        d_up = (dh * act).astype(BF16)
        hid_out[i] = hid
        d_gu_out[i, 0] = d_gate
        d_gu_out[i, 1] = d_up
        acc_dh2 = acc_dh2 + dot(d_gate, w_gate, 1, 0) + dot(d_up, w_up, 1, 0)
        acc_y = acc_y + dot(hid, w_down, 1, 0)
    put_rows(dh2_out, acc_dh2)
    for r in range(4):
        y_out[r] = acc_y[r * rows : (r + 1) * rows].astype(BF16)


def ffn_grad_kernel(windows, ins, outs):
    hid, d_gu = ins[:windows], ins[windows : 2 * windows]
    h2_all = rows_of(ins[2 * windows : 3 * windows])
    dy_all = rows_of(ins[3 * windows : 4 * windows])
    core = ins[-1][0]
    for out, slot, block in ((1, 0, 1 - core), (1, 1, 3), (0, 0, core), (0, 1, 2)):
        for part in range(2):
            d_block = jnp.concatenate([r[block, part] for r in d_gu], axis=0)
            outs[out][slot, part] = dot(d_block.T, h2_all, 1, 0).astype(BF16)
        hid_block = jnp.concatenate([r[block] for r in hid], axis=0)
        outs[out][slot, 2] = dot(hid_block.T, dy_all, 1, 0).astype(BF16)


def load_keys(own, pair, bias):
    keys = jnp.concatenate([r[HD : 2 * HD, :] for r in own] + [pair[i, :HD] for i in range(4)], axis=1)
    values = jnp.concatenate([r[2 * HD :, :] for r in own] + [pair[i, HD:] for i in range(4)], axis=1)
    row = lax.broadcasted_iota(jnp.int32, (16, keys.shape[1]), 0)
    extra = jnp.where(row == 0, bias[...], 0.0).astype(BF16)
    return keys, values, jnp.concatenate([keys, extra], axis=0)


def with_one(queries):
    row = lax.broadcasted_iota(jnp.int32, (16, queries.shape[1]), 0)
    return jnp.concatenate([queries, jnp.where(row == 0, 1.0, 0.0).astype(BF16)], axis=0)


def attend_kernel(ins, outs):
    own, pair, bias = ins[0:4], ins[4], ins[5]
    out, wide, lse = outs[0:4], outs[4], outs[5]
    _, values, keys_bias = load_keys(own, pair, bias)
    keys_rows = keys_bias.T
    for i in range(4):
        scores = dot(keys_rows, with_one(own[i][:HD, :]), 1, 0)
        top = jnp.max(scores, axis=0, keepdims=True)
        weights = jnp.exp(scores - top)
        total = jnp.sum(weights, axis=0, keepdims=True)
        attended = dot(values, weights.astype(BF16), 1, 0) * (1.0 / total)
        wide[i] = attended
        out[i][...] = attended.astype(BF16)
        lse[i] = top + jnp.log(total)


def attend_back_kernel(ins, outs):
    own, pair, bias = ins[0:4], ins[4], ins[5]
    dob, wide, lse = ins[6:10], ins[10], ins[11]
    d_own, d_pair = outs[0:4], outs[4]
    keys, values, keys_bias = load_keys(own, pair, bias)
    keys_rows = keys_bias.T
    values_rows = values.T
    dk = jnp.zeros((keys.shape[1], HD), F32)
    dv = jnp.zeros((keys.shape[1], HD), F32)
    for i in range(4):
        queries, grad = own[i][:HD, :], dob[i][...]
        scores = dot(keys_rows, with_one(queries), 1, 0)
        weights = jnp.exp(scores - lse[i])
        delta = jnp.sum(grad.astype(F32) * wide[i], axis=0, keepdims=True)
        grad_weights = dot(values_rows, grad, 1, 0)
        grad_scores = (weights * (grad_weights - delta)).astype(BF16)
        d_own[i][:HD, :] = (dot(keys, grad_scores, 1, 0) * 0.125).astype(BF16)
        dk = dk + dot(grad_scores, queries, 1, 1)
        dv = dv + dot(weights.astype(BF16), grad, 1, 1)
    dkv = jnp.concatenate([dk, dv], axis=1).T
    width = own[0].shape[1]
    for i in range(4):
        d_own[i][HD:, :] = dkv[:, i * width : (i + 1) * width].astype(BF16)
        d_pair[i] = dkv[:, (4 + i) * width : (5 + i) * width].astype(BF16)


def pick(values, index, size=1, axis=0):
    return lax.dynamic_slice_in_dim(values, index, size, axis)


Y_GROUPS = [[0, 2, 4, 6], [1, 3, 5, 7]]


def shards(hidden_in, out_grad, norm_scales, norm_shifts, w_qkv, w_out, w_gate_up, w_down, lengths):
    rows, windows, width = hidden_in.shape
    tensor = lax.axis_index("tensor")
    y, xl = tensor // 2, tensor % 2
    z = lax.axis_index("blk")
    core = lax.axis_index("dp") % 2
    tokens = 4 * rows
    ff = w_down.shape[0]
    half = ff // 2

    x_own = [hidden_in[:, w, :] for w in range(windows)]
    dy_own = [out_grad[:, w, :] for w in range(windows)]
    x_all = [gather_y(v) for v in x_own]
    dy_abs = lax.all_gather(
        out_grad.transpose(1, 0, 2), "tensor", axis=0, axis_index_groups=Y_GROUPS
    )

    heads_own = jnp.concatenate(
        [
            w_qkv.reshape(3, width, 2, HD).transpose(2, 0, 3, 1).reshape(2, 3 * HD, width),
            w_out.reshape(2, HD, width),
        ],
        axis=1,
    )
    heads_recv = send_x(pick(heads_own, core), (-1, 1))
    heads_four = jnp.concatenate([heads_own, heads_recv, send_core(heads_recv)], axis=0)
    gate_up_own = w_gate_up.transpose(0, 2, 1).reshape(2, 2, half, width)
    units_own = jnp.concatenate([gate_up_own, w_down.reshape(1, 2, half, width)], axis=0)
    units_own = units_own.transpose(1, 0, 2, 3)
    units_recv = send_x(pick(units_own, core)[0], (-1, 1))
    units_other = send_core(units_recv)

    heads_rel = []
    for r in range(4):
        head = (z + r) % 4
        place = jnp.where(head // 2 == xl, head % 2, 2 + ((head % 2) ^ core))
        heads_rel.append(pick(heads_four, place))
    heads_rel = jnp.concatenate(heads_rel, axis=0)
    w_in = heads_rel[:, : 3 * HD].reshape(12 * HD, width)
    w_back = heads_rel[:, 3 * HD :].reshape(4 * HD, width)

    lane = jnp.arange(tokens, dtype=jnp.int32)
    within = ((y + lane // rows) % 4) * (2 * rows) + lane % rows
    inverse = 10000.0 ** (-(jnp.arange(HD // 2, dtype=F32) * 2.0) / HD)
    angles = inverse[:, None] * (z * (8 * rows) + within + xl * rows).astype(F32)[None, :]
    cosine, sine = jnp.cos(angles), jnp.sin(angles)
    key_places = jnp.concatenate(
        [
            ((z - r) % 4) * (8 * rows) + within + side * rows
            for side in (xl, 1 - xl)
            for r in range(4)
        ]
    )
    bias = [
        jnp.where(key_places < lengths[w], 0.0, MASKED).astype(F32)[None, :] for w in range(windows)
    ]

    gain = [norm_scales[i : i + 1] for i in range(2)]
    offset = [norm_shifts[i : i + 1] for i in range(2)]
    y_index = jnp.full((1,), y, jnp.int32)
    z_index = jnp.full((1,), z, jnp.int32)
    flag = jnp.full((1,), core, jnp.int32)
    heads_at = (z + jnp.arange(4, dtype=jnp.int32)) % 4
    slots = jnp.where(heads_at // 2 == xl, 0, 1) + jnp.where(heads_at % 2 == core, 0, 2)
    piece, head_piece = ((rows, width), BF16), ((HD, tokens), BF16)
    triple = ((3 * HD, tokens), BF16)
    work = 2 * tokens * width * tokens

    keep = [dict() for _ in range(windows)]
    order = []

    def after(value):
        order.append(value)

    def last():
        return order[-1:]

    def project(w, k):
        *sent, k["normed"] = call(
            project_kernel, "project", [*x_all[w], w_in, gain[0], offset[0], cosine, sine],
            [triple] * 4 + [((tokens, width), BF16)], 3 * work, last(), 12,
        )
        after(sent[0])
        k["own"] = gather_z(sent)
        k["pair"] = send_pair(jnp.stack([v[HD:] for v in k["own"]]))

    def attend(w, k):
        *out, k["wide"], k["lse"] = call(
            attend_kernel, "attend", [*k["own"], k["pair"], bias[w]],
            [head_piece] * 4 + [((4, HD, tokens), F32), ((4, 1, tokens), F32)],
            128 * HD * tokens * tokens, last(), 20,
        )
        after(out[0])
        k["out"] = scatter_z(out)

    def out_project(w, k):
        *parts, k["ob"] = call(
            out_kernel, "out_project", [*k["out"], w_back],
            [piece] * 4 + [((4 * HD, tokens), BF16)], work, last(),
        )
        after(parts[0])
        k["attn"] = scatter_y(parts)

    def middle(w, k):
        k["middle"], h2 = call(
            middle_kernel, "middle", [*k["attn"], x_own[w], gain[1], offset[1]],
            [((rows, width), F32), piece], 0, last(),
        )
        after(h2)
        k["h2"] = gather_y(h2)

    def feed_forward(w, k):
        *parts, k["y"], k["hid"], k["d_gu"], k["h2_all"], k["dy_all"] = call(
            functools.partial(ffn_kernel, w), "ffn",
            [*k["h2"], dy_abs, units_own, units_recv, units_other, y_index],
            [piece] * 4
            + [((4, rows, width), BF16), ((4, tokens, half), BF16), ((4, 2, tokens, half), BF16)]
            + [((tokens, width), BF16)] * 2,
            24 * work, last(), 24,
        )
        after(parts[0])
        k["dh2"] = scatter_y(parts)

    def middle_back(w, k):
        k["dx2"], da, k["sums"] = call(
            middle_back_kernel, "middle_back", [*k["dh2"], k["middle"], dy_own[w], gain[1]],
            [((rows, width), F32), piece, ((2, width), F32)], 0, last(),
        )
        after(da)
        k["da"] = gather_y(da)

    def out_back(w, k):
        *parts, k["da_all"] = call(
            out_back_kernel, "out_back", [*k["da"], w_back],
            [head_piece] * 4 + [((tokens, width), BF16)], work, last(),
        )
        after(parts[0])
        k["dob"] = gather_z(parts)

    def attend_back(w, k):
        *d_own, d_pair = call(
            attend_back_kernel, "attend_back",
            [*k["own"], k["pair"], bias[w], *k["dob"], k["wide"], k["lse"]],
            [triple] * 4 + [((4, 2 * HD, tokens), BF16)],
            320 * HD * tokens * tokens, last(), 28,
        )
        after(d_pair)
        k["d_own"], k["d_pair"] = d_own, send_pair(d_pair)

    def merge(w, k):
        parts = call(merge_kernel, "merge", [*k["d_own"], k["d_pair"]], [triple] * 4, 0, last())
        after(parts[0])
        k["d_sent"] = scatter_z(parts)

    def project_back(w, k):
        *parts, k["d_proj"] = call(
            project_back_kernel, "project_back", [*k["d_sent"], w_in, cosine, sine],
            [piece] * 4 + [((12 * HD, tokens), BF16)], 3 * work, last(),
        )
        after(parts[0])
        k["dh1"] = scatter_y(parts)

    def input_back(w, k):
        (k["grad_in"],) = call(
            input_back_kernel, "input_back", [*k["dh1"], x_own[w], k["dx2"], gain[0]],
            [piece], 0, last(),
        )
        after(k["grad_in"])

    def ffn_grads():
        kept, given = call(
            functools.partial(ffn_grad_kernel, windows), "ffn_grad",
            [k[name] for name in ("hid", "d_gu", "h2_all", "dy_all") for k in keep] + [flag],
            [((2, 3, half, width), BF16)] * 2, 12 * windows * work, last(), 16,
        )
        after(kept)
        return kept, given

    def out_grads():
        (total,) = call(
            out_grad_kernel, "out_grads", [v for k in keep for v in (k["ob"], k["da_all"])],
            [((4 * HD, width), F32)], windows * work, last(),
        )
        after(total)
        return total

    def heads_part():
        total, sums = call(
            heads_part_kernel, "heads_part",
            [v for k in keep[:-1] for v in (k["d_proj"], k["normed"])],
            [((12 * HD, width), F32), ((12 * HD, 128), F32)], 6 * work, last(),
        )
        after(total)
        return total, sums

    def heads_last(part, part_sum):
        wide = ((2, 4, HD + 16, width), BF16)
        kept, given = call(
            heads_kernel, "heads_last",
            [keep[-1]["d_proj"], keep[-1]["normed"], part, part_sum, g_back, w_in, gain[0], offset[0], slots]
            + [k["sums"] for k in keep],
            [wide, wide], 3 * work, last(), 20,
        )
        after(kept)
        return kept, given

    def add_core(kept, given, deps):
        shape = (kept.shape[1:], BF16)
        own, far = call(heads_core_kernel, "add_core", [kept, given], [shape] * 2, 0, deps)
        after(own)
        return own, far

    def rounds(stage):
        for w in range(windows):
            stage(w, keep[w])

    for stage in (project, attend, out_project, middle, feed_forward, middle_back):
        rounds(stage)
    units, units_given = ffn_grads()
    units_given = send_core(units_given)
    rounds(out_back)
    g_back = out_grads()
    y_parts = call(
        stack_kernel, "stack", [k["y"] for k in keep],
        [((windows * rows, width), BF16)] * 4, 0, last(),
    )
    after(y_parts[0])
    y_parts = scatter_y(y_parts)

    attend_back(0, keep[0])
    units, units_far = add_core(units, units_given, last())
    units_far = send_x(units_far, (-1, 1))
    attend_back(1, keep[1])
    attend_back(2, keep[2])
    merge(0, keep[0])
    merge(1, keep[1])
    (result,) = call(
        result_kernel, "result", y_parts + [k["middle"] for k in keep],
        [((windows, rows, width), BF16)], 0, last(),
    )
    after(result)
    merge(2, keep[2])
    (units,) = call(sum_kernel, "add", [units, units_far], [(units.shape, BF16)], 0, last())
    after(units)
    units = lax.psum_scatter(units.reshape(-1, width), "blk", scatter_dimension=0, tiled=True)

    project_back(0, keep[0])
    project_back(1, keep[1])
    part = heads_part()
    project_back(2, keep[2])
    heads, heads_given = heads_last(*part)
    heads_given = send_core(heads_given)
    input_back(0, keep[0])
    heads, heads_far = add_core(heads, heads_given, last())
    heads_far = send_x(heads_far, (-1, 1))
    input_back(1, keep[1])
    input_back(2, keep[2])
    units_far = send_far(units)
    chunk = ((HD + 16, width), BF16)
    parts = call(heads_pair_kernel, "add_pair", [heads, heads_far, z_index], [chunk] * 4, 0, last())
    after(parts[0])
    parts = [parts[0]] + [send_z(parts[r], r) for r in (1, 2, 3)]
    (units,) = call(sum_kernel, "add", [units, units_far], [(units.shape, BF16)], 0, last())
    after(units)
    units = lax.all_gather(units, "blk", axis=0, tiled=True)
    (part,) = call(sum_kernel, "add", parts, [chunk], 0, last())
    after(part)
    (part,) = call(sum_kernel, "add", [part, send_far(part)], [chunk], 0, last())
    after(part)
    heads, small = call(
        heads_ring_kernel, "ring", [part] + [send_z(part, -r) for r in (1, 2, 3)] + [z_index],
        [((4, HD + 16, width), BF16), ((4, 1, width), F32)], 0, last(),
    )
    after(heads)
    grad_gate_up, grad_down = call(
        units_final_kernel, "units_final", [units, send_core(units), flag],
        [((2, width, ff), F32), ((ff, width), F32)], 0, last(),
    )
    after(grad_down)
    grad_qkv, grad_out = call(
        heads_final_kernel, "heads_final", [heads, send_core(heads), flag],
        [((3, width, 2 * HD), F32), ((2 * HD, width), F32)], 0, last(),
    )
    small = small.reshape(4, width)
    small = small + sum(send_y(small, r) for r in (1, 2, 3))

    return (
        result.transpose(1, 0, 2),
        jnp.stack([k["grad_in"] for k in keep], axis=1),
        grad_qkv,
        grad_out,
        grad_gate_up,
        grad_down,
        small[:2],
        small[2:],
    )


def solution(mesh):
    placed = (
        P(("blk", "tensor"), "dp", None),
        P(("blk", "tensor"), "dp", None),
        P(),
        P(),
        P(None, None, "tensor"),
        P("tensor", None),
        P(None, None, "tensor"),
        P("tensor", None),
        P("dp"),
    )
    return jax.shard_map(
        shards,
        mesh=mesh,
        in_specs=placed,
        out_specs=(
            P(("blk", "tensor"), "dp", None),
            P(("blk", "tensor"), "dp", None),
            P(None, None, "tensor"),
            P("tensor", None),
            P(None, None, "tensor"),
            P("tensor", None),
            P(),
            P(),
        ),
        check_vma=False,
    )
```

```python
import functools
import math

import jax
import jax.numpy as jnp
from jax import lax
from jax.experimental import pallas as pl
from jax.experimental.pallas import tpu as pltpu
from jax.sharding import PartitionSpec as P

HD = 64
EPSILON = 1e-05
MASKED = -1000000000.0
F32 = jnp.float32
BF16 = jnp.bfloat16
MIB = 1024 * 1024


def send_y(values, step):
    pairs = [(i, ((i // 2 + step) % 4) * 2 + i % 2) for i in range(8)]
    return lax.ppermute(values, "tensor", pairs)


def send_pair(values):
    return lax.ppermute(values, "tensor", [(i, i ^ 1) for i in range(8)])


def send_z(values, step):
    return lax.ppermute(values, "blk", [(i, (i + step) % 4) for i in range(4)])


def send_core(values):
    return lax.ppermute(values, "dp", [(i, i ^ 1) for i in range(4)])


def send_far(values):
    return lax.ppermute(values, "dp", [(i, i ^ 2) for i in range(4)])


def send_x(values, steps):
    pairs = []
    for d in range(4):
        for t in range(8):
            core = d % 2
            x = ((d // 2) * 2 + t % 2 + steps[core]) % 4
            pairs.append((d * 8 + t, ((x // 2) * 2 + core) * 8 + (t // 2) * 2 + x % 2))
    return lax.ppermute(values, ("dp", "tensor"), pairs)


def gather_y(values):
    return [values] + [send_y(values, -r) for r in (1, 2, 3)]


def add_low(a, b):
    return (a.astype(F32) + b.astype(F32)).astype(BF16)


def scatter_y(parts):
    own, next_low, next_high, far_low, far_high, before_low, before_high = parts
    right, left = send_y(far_low, 1), send_y(far_high, -1)
    right_high, left_low = send_y(next_high, 1), send_y(before_low, -1)
    right = send_y(add_low(next_low, right), 1)
    left = send_y(add_low(before_high, left), -1)
    return [own, right, right_high, left_low, left]


def gather_z(parts):
    return [parts[0]] + [send_z(parts[r], r) for r in (1, 2, 3)]


def scatter_z(parts):
    return [parts[0]] + [send_z(parts[r], -r) for r in (1, 2, 3)]


def norm_parts(values):
    mean = jnp.mean(values, axis=-1, keepdims=True)
    centred = values - mean
    inverse = lax.rsqrt(jnp.mean(centred * centred, axis=-1, keepdims=True) + EPSILON)
    return centred * inverse, inverse


def norm_back(normed, inverse, gain, cotangent):
    e = cotangent * gain
    grad = (
        e
        - jnp.mean(e, axis=-1, keepdims=True)
        - normed * jnp.mean(e * normed, axis=-1, keepdims=True)
    ) * inverse
    return grad, jnp.sum(cotangent * normed, axis=0), jnp.sum(cotangent, axis=0)


def dot(a, b, ca, cb):
    return lax.dot_general(a, b, (((ca,), (cb,)), ((), ())), preferred_element_type=F32)


def rows_of(refs):
    return jnp.concatenate([r[...] for r in refs], axis=0)


def put_rows(refs, values):
    rows = refs[0].shape[0]
    for i, ref in enumerate(refs):
        ref[...] = values[i * rows : (i + 1) * rows].astype(ref.dtype)


def call(kernel, name, inputs, outs, flops, after=(), mib=8):
    count = len(inputs)

    def body(*refs):
        kernel(refs[:count], refs[count + len(after) :])

    return pl.pallas_call(
        body,
        in_specs=[
            pl.BlockSpec(memory_space=pltpu.SMEM if v.dtype == jnp.int32 else pltpu.VMEM)
            for v in inputs
        ]
        + [pl.BlockSpec(memory_space=pl.ANY)] * len(after),
        out_specs=[pl.BlockSpec(memory_space=pltpu.VMEM)] * len(outs),
        out_shape=[jax.ShapeDtypeStruct(shape, dtype) for shape, dtype in outs],
        compiler_params=pltpu.CompilerParams(vmem_limit_bytes=mib * MIB),
        cost_estimate=pl.CostEstimate(flops=2 * flops + 2_000_000_000, bytes_accessed=4_000_000, transcendentals=0),
        name=name,
    )(*inputs, *after)


def heads_prepare_kernel(ins, outs):
    w_qkv, w_out, core = ins
    for part in range(3):
        turned = w_qkv[part].T
        for j in range(2):
            outs[0][j, part * HD : (part + 1) * HD] = turned[j * HD : (j + 1) * HD]
    for j in range(2):
        outs[0][j, 3 * HD :] = w_out[j * HD : (j + 1) * HD]
    outs[1][...] = outs[0][core[0]]


def heads_order_kernel(ins, outs):
    own, recv, other, places = ins
    for r in range(4):
        place = places[r]
        head = jnp.where(place < 2, own[jnp.minimum(place, 1)], jnp.where(place == 2, recv[...], other[...]))
        outs[0][3 * HD * r : 3 * HD * (r + 1)] = head[: 3 * HD]
        outs[1][HD * r : HD * (r + 1)] = head[3 * HD :]


def units_prepare_kernel(ins, outs):
    w_gate_up, w_down, core = ins
    half = w_down.shape[0] // 2
    for j in range(2):
        for part in range(2):
            outs[0][j, part] = w_gate_up[part, :, j * half : (j + 1) * half].T
        outs[0][j, 2] = w_down[j * half : (j + 1) * half]
    outs[1][...] = outs[0][core[0]]


def y_total(refs):
    first = jnp.concatenate([refs[1][...], refs[2][...]], axis=0).astype(F32)
    second = jnp.concatenate([refs[3][...], refs[4][...]], axis=0).astype(F32)
    return refs[0][...].astype(F32) + first + second


def window_rows(refs, j, rows):
    return jnp.concatenate([r[j * rows : (j + 1) * rows] for r in refs], axis=0)


def put_parts(refs, parts):
    refs[0][...] = parts[0].astype(BF16)
    half = refs[1].shape[0]
    for i, part in enumerate(parts[1:]):
        refs[2 * i + 1][...] = part[:half].astype(BF16)
        refs[2 * i + 2][...] = part[half:].astype(BF16)


def put_window_parts(refs, products):
    rows = products[0].shape[0] // 4
    put_parts(
        refs,
        [
            jnp.concatenate([v[r * rows : (r + 1) * rows] for v in products], axis=0)
            for r in range(4)
        ],
    )


def project_kernel(window, ins, outs):
    w_in, gain, offset, cosine, sine = ins[4:9]
    rows = outs[0].shape[1] // 4
    c, s = cosine[...], sine[...]
    half = HD // 2
    normed, _ = norm_parts(window_rows(ins[:4], window, rows).astype(F32))
    outs[4][...] = normed.astype(BF16)
    h1 = (normed * gain[...] + offset[...]).astype(BF16)
    proj = dot(w_in[...], h1, 1, 1)
    for r in range(4):
        for part in range(3):
            at = (3 * r + part) * HD
            first, second = proj[at : at + half], proj[at + half : at + HD]
            if part < 2:
                first, second = first * c - second * s, second * c + first * s
            if part == 0:
                first, second = first * 0.125, second * 0.125
            outs[r][part * HD : part * HD + half, :] = first.astype(BF16)
            outs[r][part * HD + half : (part + 1) * HD, :] = second.astype(BF16)


def stack_kernel(ins, outs):
    for r in range(4):
        outs[0][r] = ins[r][HD:, :]


def join_kernel(ins, outs):
    outs[0][...] = rows_of(ins)


def out_kernel(ins, outs):
    ob = [r[...] for r in ins[:2]] + [rows_of(ins[2:6])]
    outs[7][...] = ob[2]
    put_window_parts(outs[:7], [dot(v.T, ins[6][...], 1, 0) for v in ob])


def middle_kernel(ins, outs):
    middle = y_total(ins[:5]) + ins[5][...].astype(F32)
    normed, _ = norm_parts(middle)
    outs[0][...] = middle
    outs[1][...] = (normed * ins[6][...] + ins[7][...]).astype(BF16)


def middle_back_kernel(ins, outs):
    dh2 = ins[0][...] + ins[1][...].astype(F32)
    normed, inv = norm_parts(ins[2][...])
    back, g_scale, g_shift = norm_back(normed, inv, ins[4][...], dh2)
    dx2 = ins[3][...].astype(F32) + back
    outs[0][...] = dx2
    outs[1][...] = dx2.astype(BF16)
    outs[2][...] = jnp.concatenate([g_scale[None], g_shift[None]], axis=0)


def out_back_kernel(window, ins, outs):
    da = window_rows(ins[:4], window, outs[0].shape[1] // 4)
    outs[4][...] = da
    put_rows(outs[:4], dot(ins[4][...], da, 1, 1))


def merge_kernel(ins, outs):
    for r in range(4):
        outs[r][:HD, :] = ins[r][:HD, :]
        total = ins[r][HD:, :].astype(F32) + ins[4][r].astype(F32)
        outs[r][HD:, :] = total.astype(BF16)


def project_back_kernel(ins, outs):
    w_in, cosine, sine = ins[-3:]
    c, s = cosine[...], sine[...]
    half = HD // 2
    products = []
    for j in range(len(ins) // 4):
        pieces = []
        for r in range(4):
            grads = ins[4 * j + r]
            for part in range(2):
                first = grads[part * HD : part * HD + half, :].astype(F32)
                second = grads[part * HD + half : (part + 1) * HD, :].astype(F32)
                pieces.append((first * c + second * s).astype(BF16))
                pieces.append((second * c - first * s).astype(BF16))
            pieces.append(grads[2 * HD :, :])
        d_proj = jnp.concatenate(pieces, axis=0)
        outs[7][j] = d_proj
        products.append(dot(d_proj.T, w_in[...], 1, 0))
    put_window_parts(outs[:7], products)


def input_back_kernel(ins, outs):
    dh1 = y_total(ins[:5])
    normed, inv = norm_parts(ins[5][...].astype(F32))
    back, _, _ = norm_back(normed, inv, ins[7][...], dh1)
    outs[0][...] = (ins[6][...] + back).astype(BF16)


def heads_kernel(ins, outs):
    d_proj, back, w_in, gain, offset, slots, second = ins[:7]
    total, sums = 0.0, 0.0
    for j, normed in enumerate(ins[7:]):
        total = total + dot(d_proj[j], normed[...], 1, 0)
        sums = sums + jnp.sum(d_proj[j].astype(F32), axis=1, keepdims=True)
    g_in = (total * gain[...] + sums * offset[...]).astype(BF16)
    wide = w_in[...].astype(F32)
    small = [
        jnp.sum(wide * total, axis=0, keepdims=True),
        second[:1, :],
        jnp.sum(wide * sums, axis=0, keepdims=True),
        second[1:, :],
    ]
    row = lax.broadcasted_iota(jnp.int32, (16, g_in.shape[1]), 0)
    small = [jnp.where(row == 0, v, 0.0).astype(BF16) for v in small]

    def put(out, slot, r):
        for chunk in range(4):
            if chunk < 3:
                rows = g_in[3 * HD * r + HD * chunk : 3 * HD * r + HD * (chunk + 1)]
            else:
                rows = back[HD * r : HD * (r + 1)].astype(BF16)
            out[slot, chunk, :HD] = rows
            out[slot, chunk, HD:] = small[chunk]

    for r in range(4):
        slot = slots[r]

        @pl.when(slot < 2)
        def _(slot=slot, r=r):
            put(outs[0], slot, r)

        @pl.when(slot >= 2)
        def _(slot=slot, r=r):
            put(outs[1], slot - 2, r)


def heads_core_kernel(ins, outs):
    for i in range(2):
        outs[i][...] = (ins[0][i].astype(F32) + ins[1][i].astype(F32)).astype(BF16)


def heads_pair_kernel(ins, outs):
    for r in range(4):
        chunk = lax.rem(ins[2][0] + r, 4)
        outs[r][...] = (ins[0][chunk].astype(F32) + ins[1][chunk].astype(F32)).astype(BF16)


def sum_kernel(ins, outs):
    outs[0][...] = sum(r[...].astype(F32) for r in ins).astype(outs[0].dtype)


def heads_ring_kernel(ins, outs):
    for r in range(4):
        chunk = lax.rem(ins[4][0] + r, 4)
        outs[0][chunk] = ins[r][...]
    for r in range(4):
        outs[1][lax.rem(ins[4][0] + r, 4)] = ins[r][HD : HD + 1].astype(F32)


def out_grad_kernel(ins, outs):
    outs[0][...] = sum(dot(ob[...], da[...], 1, 0) for ob, da in zip(ins[:3], ins[3:]))


def by_core(core, mine, other):
    low = jnp.where(core == 0, mine, other).astype(F32)
    high = jnp.where(core == 0, other, mine).astype(F32)
    return low, high


def units_final_kernel(ins, outs):
    low, high = by_core(ins[2][0], ins[0][...], ins[1][...])
    half = low.shape[0] // 3
    for side, values in enumerate((low, high)):
        for part in range(2):
            outs[0][part, :, side * half : (side + 1) * half] = values[
                part * half : (part + 1) * half
            ].T
        outs[1][side * half : (side + 1) * half] = values[2 * half :]


def heads_final_kernel(ins, outs):
    low, high = by_core(ins[2][0], ins[0][:, :HD], ins[1][:, :HD])
    for part in range(3):
        outs[0][part] = jnp.concatenate([low[part], high[part]], axis=0).T
    outs[1][...] = jnp.concatenate([low[3], high[3]], axis=0)


def parts_kernel(ins, outs):
    put_parts(outs, [r[...] for r in ins])


def result_kernel(ins, outs):
    outs[0][...] = (y_total(ins[:5]) + ins[5][...]).astype(BF16)


def ffn_kernel(r, ins, outs):
    dy_in, own, recv, other, y = ins[-5:]
    dh2_out, y_out, hid_out, d_gu_out = outs[:4]
    h2 = ins[0][...]
    dy = dy_in[lax.rem(y[0] + r, 4)]
    acc_dh2, acc_y = 0.0, 0.0
    for i, (w_gate, w_up, w_down) in enumerate(
        [[own[j, part] for part in range(3)] for j in range(2)]
        + [[ref[part] for part in range(3)] for ref in (recv, other)]
    ):
        gate = dot(h2, w_gate, 1, 1)
        up = dot(h2, w_up, 1, 1)
        dh = dot(dy, w_down, 1, 1)
        sig = 1.0 / (1.0 + jnp.exp(-gate))
        act = gate * sig
        hid = (act * up).astype(BF16)
        d_gate = (dh * up * (sig + act * (1.0 - sig))).astype(BF16)
        d_up = (dh * act).astype(BF16)
        hid_out[i] = hid
        d_gu_out[i, 0] = d_gate
        d_gu_out[i, 1] = d_up
        acc_dh2 = acc_dh2 + dot(d_gate, w_gate, 1, 0) + dot(d_up, w_up, 1, 0)
        acc_y = acc_y + dot(hid, w_down, 1, 0)
    dh2_out[...] = acc_dh2.astype(BF16)
    y_out[...] = acc_y.astype(BF16)


def ffn_grad_kernel(ins, outs):
    hid, d_gu, dy, flags = ins[:4], ins[4:8], ins[12], ins[13]
    h2_all = rows_of(ins[8:12])
    core, y = flags[0], flags[1]
    dy_all = jnp.concatenate([dy[lax.rem(y + r, 4)] for r in range(4)], axis=0)
    for out, slot, block in ((1, 0, 1 - core), (1, 1, 3), (0, 0, core), (0, 1, 2)):
        for part in range(2):
            d_block = jnp.concatenate([r[block, part] for r in d_gu], axis=0)
            outs[out][slot, part] = dot(d_block.T, h2_all, 1, 0).astype(BF16)
        hid_block = jnp.concatenate([r[block] for r in hid], axis=0)
        outs[out][slot, 2] = dot(hid_block.T, dy_all, 1, 0).astype(BF16)


def load_keys(own, pair, places):
    keys = jnp.concatenate([r[HD : 2 * HD, :] for r in own] + [pair[i, :HD] for i in range(4)], axis=1)
    values = jnp.concatenate([r[2 * HD :, :] for r in own] + [pair[i, HD:] for i in range(4)], axis=1)
    z, y, xl = places[0], places[1], places[2]
    tokens = own[0].shape[1]
    rows = tokens // 4
    lane = lax.broadcasted_iota(jnp.int32, (1, 8 * tokens), 1)
    source, within = lane // tokens, lane % tokens
    side = jnp.where(source < 4, xl, 1 - xl)
    at = ((z + 4 - source % 4) % 4) * (8 * rows) + ((y + within // rows) % 4) * (2 * rows)
    at = at + side * rows + within % rows
    bias = jnp.where(at < places[3], 0.0, MASKED)
    row = lax.broadcasted_iota(jnp.int32, (16, 8 * tokens), 0)
    extra = jnp.where(row == 0, bias, 0.0).astype(BF16)
    return keys, values, jnp.concatenate([keys, extra], axis=0)


def with_one(queries):
    row = lax.broadcasted_iota(jnp.int32, (16, queries.shape[1]), 0)
    return jnp.concatenate([queries, jnp.where(row == 0, 1.0, 0.0).astype(BF16)], axis=0)


def attend_kernel(ins, outs):
    own, pair, places = ins[0:4], ins[4], ins[5]
    out, wide, lse = outs[0:4], outs[4], outs[5]
    _, values, keys_bias = load_keys(own, pair, places)
    keys_rows = keys_bias.T
    for i in range(4):
        scores = dot(keys_rows, with_one(own[i][:HD, :]), 1, 0)
        top = jnp.max(scores, axis=0, keepdims=True)
        weights = jnp.exp(scores - top)
        total = jnp.sum(weights, axis=0, keepdims=True)
        attended = dot(values, weights.astype(BF16), 1, 0) * (1.0 / total)
        wide[i] = attended
        out[i][...] = attended.astype(BF16)
        lse[i] = top + jnp.log(total)


def attend_back_kernel(ins, outs):
    own, pair, places = ins[0:4], ins[4], ins[5]
    dob, wide, lse = ins[6:10], ins[10], ins[11]
    d_own, d_pair = outs[0:4], outs[4]
    width = own[0].shape[1]
    keys, values, keys_bias = load_keys(own, pair, places)
    keys_rows = keys_bias.T
    values_rows = values.T
    dk = jnp.zeros((keys.shape[1], HD), F32)
    dv = jnp.zeros((keys.shape[1], HD), F32)
    for i in range(4):
        queries, grad = own[i][:HD, :], dob[i][...]
        scores = dot(keys_rows, with_one(queries), 1, 0)
        weights = jnp.exp(scores - lse[i])
        delta = jnp.sum(grad.astype(F32) * wide[i], axis=0, keepdims=True)
        grad_weights = dot(values_rows, grad, 1, 0)
        grad_scores = (weights * (grad_weights - delta)).astype(BF16)
        d_own[i][:HD, :] = (dot(keys, grad_scores, 1, 0) * 0.125).astype(BF16)
        dk = dk + dot(grad_scores, queries, 1, 1)
        dv = dv + dot(weights.astype(BF16), grad, 1, 1)
    dkv = jnp.concatenate([dk, dv], axis=1).T
    for i in range(4):
        d_own[i][HD:, :] = dkv[:, i * width : (i + 1) * width].astype(BF16)
        d_pair[i] = dkv[:, (4 + i) * width : (5 + i) * width].astype(BF16)


Y_GROUPS = [[0, 2, 4, 6], [1, 3, 5, 7]]


def shards(hidden_in, out_grad, norm_scales, norm_shifts, w_qkv, w_out, w_gate_up, w_down, lengths):
    rows, windows, width = hidden_in.shape
    tensor = lax.axis_index("tensor")
    y, xl = tensor // 2, tensor % 2
    z = lax.axis_index("blk")
    core = lax.axis_index("dp") % 2
    tokens = 4 * rows
    ff = w_down.shape[0]
    half = ff // 2

    order = []

    x_rows = hidden_in.transpose(1, 0, 2).reshape(windows * rows, width)
    dy_rows = out_grad.transpose(1, 0, 2).reshape(windows * rows, width)
    x_all = gather_y(x_rows)
    dy_abs = lax.all_gather(dy_rows, "tensor", axis=0, axis_index_groups=Y_GROUPS)

    y_index = jnp.full((1,), y, jnp.int32)
    z_index = jnp.full((1,), z, jnp.int32)
    flag = jnp.full((1,), core, jnp.int32)
    core_y = jnp.stack([core, y]).astype(jnp.int32)
    heads_at = (z + jnp.arange(4, dtype=jnp.int32)) % 4
    slots = jnp.where(heads_at // 2 == xl, 0, 1) + jnp.where(heads_at % 2 == core, 0, 2)
    places = jnp.where(heads_at // 2 == xl, heads_at % 2, 2 + ((heads_at % 2) ^ core))
    here = [jnp.stack([z, y, xl, lengths[w]]).astype(jnp.int32) for w in range(windows)]

    heads_own, heads_recv = call(
        heads_prepare_kernel, "heads_prepare", [w_qkv, w_out, flag],
        [((2, 4 * HD, width), BF16), ((4 * HD, width), BF16)], 0,
    )
    heads_recv = send_x(heads_recv, (-1, 1))
    units_own, units_recv = call(
        units_prepare_kernel, "units_prepare", [w_gate_up, w_down, flag],
        [((2, 3, half, width), BF16), ((3, half, width), BF16)], 0, [heads_own], 12,
    )
    w_in, w_back = call(
        heads_order_kernel, "heads_order", [heads_own, heads_recv, send_core(heads_recv), places],
        [((12 * HD, width), BF16), ((4 * HD, width), BF16)], 0, [units_own],
    )
    units_recv = send_x(units_recv, (-1, 1))
    units_other = send_core(units_recv)

    lane = jnp.arange(tokens, dtype=jnp.int32)
    within = ((y + lane // rows) % 4) * (2 * rows) + lane % rows
    inverse = 10000.0 ** (-(jnp.arange(HD // 2, dtype=F32) * 2.0) / HD)
    angles = inverse[:, None] * (z * (8 * rows) + within + xl * rows).astype(F32)[None, :]
    cosine, sine = jnp.cos(angles), jnp.sin(angles)

    gain = [norm_scales[i : i + 1] for i in range(2)]
    offset = [norm_shifts[i : i + 1] for i in range(2)]
    work = 2 * tokens * width * tokens
    piece, piece_wide = ((windows * rows, width), BF16), ((windows * rows, width), F32)
    head_piece, triple = ((HD, tokens), BF16), ((3 * HD, tokens), BF16)
    each = range(windows)

    def after(value):
        order.append(value)

    def last():
        return order[-1:]

    def add_core(kept, given, deps):
        shape = (kept.shape[1:], BF16)
        own, far = call(heads_core_kernel, "add_core", [kept, given], [shape] * 2, 0, deps)
        after(own)
        return own, far

    def run(kernel, name, inputs, outs, flops=0, mib=8):
        out = call(kernel, name, inputs, outs, flops, last(), mib)
        after(out[0])
        return out

    whole_and_halves = [piece] + [((windows * rows // 2, width), BF16)] * 6
    own, pair, normed_all, out, wide, lse, ob = ([None] * windows for _ in range(7))

    def project(w):
        *sent, normed_all[w] = run(
            functools.partial(project_kernel, w), "project",
            [*x_all, w_in, gain[0], offset[0], cosine, sine],
            [triple] * 4 + [((tokens, width), BF16)], 3 * work, 10,
        )
        own[w] = gather_z(sent)

    def stack(w):
        (pair[w],) = run(stack_kernel, "stack", own[w], [((4, 2 * HD, tokens), BF16)])
        pair[w] = send_pair(pair[w])

    def attend(w):
        *parts, wide[w], lse[w] = run(
            attend_kernel, "attend", [*own[w], pair[w], here[w]],
            [head_piece] * 4 + [((4, HD, tokens), F32), ((4, 1, tokens), F32)],
            128 * HD * tokens * tokens, 10,
        )
        out[w] = scatter_z(parts)

    def join(w):
        (ob[w],) = run(join_kernel, "join", out[w], [((4 * HD, tokens), BF16)])

    for stage, w in (
        (project, 0), (project, 1), (project, 2), (stack, 0), (stack, 1), (attend, 0), (stack, 2),
        (attend, 1), (join, 0), (attend, 2), (join, 1),
    ):
        stage(w)
    *parts, ob[2] = run(
        out_kernel, "out_project", [*ob[:2], *out[2], w_back],
        whole_and_halves + [((4 * HD, tokens), BF16)], 3 * work,
    )
    middle, h2 = run(
        middle_kernel, "middle", [*scatter_y(parts), x_rows, gain[1], offset[1]], [piece_wide, piece]
    )

    h2_all = gather_y(h2)
    dh2, y_part, hid, d_gu = [None] * 4, [None] * 4, [None] * 4, [None] * 4
    for r in (0, 1, 3, 2):
        dh2[r], y_part[r], hid[r], d_gu[r] = run(
            functools.partial(ffn_kernel, r), "ffn",
            [h2_all[r], dy_abs, units_own, units_recv, units_other, y_index],
            [piece, piece, ((4, windows * rows, half), BF16), ((4, 2, windows * rows, half), BF16)],
            18 * work, 10,
        )
        if r:
            dh2[r] = send_y(dh2[r], r)
    (dh2_near,) = run(sum_kernel, "add", [dh2[0], dh2[1], dh2[3]], [piece_wide])
    units, units_given = run(
        ffn_grad_kernel, "ffn_grad", [*hid, *d_gu, *h2_all, dy_abs, core_y],
        [((2, 3, half, width), BF16)] * 2, 36 * work, 10,
    )
    units_given = send_core(units_given)
    dx2, da, norm_sums = run(
        middle_back_kernel, "middle_back", [dh2_near, dh2[2], middle, dy_rows, gain[1]],
        [piece_wide, piece, ((2, width), F32)],
    )
    da_all = gather_y(da)
    units, units_far = add_core(units, units_given, last())
    units_far = send_x(units_far, (-1, 1))

    dob, da_rows = [None] * windows, [None] * windows
    for w in each:
        *parts, da_rows[w] = run(
            functools.partial(out_back_kernel, w), "out_back", [*da_all, w_back],
            [head_piece] * 4 + [((tokens, width), BF16)], work,
        )
        dob[w] = gather_z(parts)
    (g_back,) = run(
        out_grad_kernel, "out_grads", [*ob, *da_rows], [((4 * HD, width), F32)], 3 * work
    )
    y_part = run(parts_kernel, "parts", y_part, whole_and_halves)
    y_part = scatter_y(y_part)
    d_own, d_pair = [None] * windows, [None] * windows
    d_sent = [None] * windows

    def attend_back(w):
        *d_own[w], d_pair[w] = run(
            attend_back_kernel, "attend_back",
            [*own[w], pair[w], here[w], *dob[w], wide[w], lse[w]],
            [triple] * 4 + [((4, 2 * HD, tokens), BF16)], 320 * HD * tokens * tokens, 14,
        )
        d_pair[w] = send_pair(d_pair[w])

    def merge(w):
        parts = run(merge_kernel, "merge", [*d_own[w], d_pair[w]], [triple] * 4)
        d_sent[w] = scatter_z(parts)

    attend_back(0)
    (units,) = run(sum_kernel, "add", [units, units_far], [(units.shape, BF16)])
    units = lax.psum_scatter(units.reshape(-1, width), "blk", scatter_dimension=0, tiled=True)
    attend_back(1)
    merge(0)
    attend_back(2)
    merge(1)
    merge(2)
    (result,) = run(result_kernel, "result", [*y_part, middle], [piece])
    (units,) = run(sum_kernel, "add", [units, send_far(units)], [(units.shape, BF16)])
    units = lax.all_gather(units, "blk", axis=0, tiled=True)
    *parts, d_proj = run(
        project_back_kernel, "project_back", [v for k in d_sent for v in k] + [w_in, cosine, sine],
        whole_and_halves + [((windows, 12 * HD, tokens), BF16)], 9 * work, 10,
    )
    dh1 = scatter_y(parts)
    wide_heads = ((2, 4, HD + 16, width), BF16)
    heads, heads_given = run(
        heads_kernel, "heads",
        [d_proj, g_back, w_in, gain[0], offset[0], slots, norm_sums, *normed_all],
        [wide_heads, wide_heads], 9 * work, 10,
    )
    heads, heads_far = add_core(heads, send_core(heads_given), last())
    heads_far = send_x(heads_far, (-1, 1))
    (grad_in,) = run(input_back_kernel, "input_back", [*dh1, x_rows, dx2, gain[0]], [piece])
    chunk = ((HD + 16, width), BF16)
    parts = run(heads_pair_kernel, "add_pair", [heads, heads_far, z_index], [chunk] * 4)
    parts = [parts[0]] + [send_z(parts[r], r) for r in (1, 2, 3)]
    (part,) = run(sum_kernel, "add", parts, [chunk])
    (part,) = run(sum_kernel, "add", [part, send_far(part)], [chunk])
    ring = [part] + [send_z(part, -r) for r in (1, 2, 3)]
    grad_gate_up, grad_down = run(
        units_final_kernel, "units_final", [units, send_core(units), flag],
        [((2, width, ff), F32), ((ff, width), F32)],
    )
    heads, small = run(
        heads_ring_kernel, "ring", [*ring, z_index],
        [((4, HD + 16, width), BF16), ((4, 1, width), F32)],
    )
    grad_qkv, grad_out = run(
        heads_final_kernel, "heads_final", [heads, send_core(heads), flag],
        [((3, width, 2 * HD), F32), ((2 * HD, width), F32)],
    )
    small = small.reshape(4, width)
    small = small + sum(send_y(small, r) for r in (1, 2, 3))

    return (
        result.reshape(windows, rows, width).transpose(1, 0, 2),
        grad_in.reshape(windows, rows, width).transpose(1, 0, 2),
        grad_qkv,
        grad_out,
        grad_gate_up,
        grad_down,
        small[:2],
        small[2:],
    )


def solution(mesh):
    placed = (
        P(("blk", "tensor"), "dp", None),
        P(("blk", "tensor"), "dp", None),
        P(),
        P(),
        P(None, None, "tensor"),
        P("tensor", None),
        P(None, None, "tensor"),
        P("tensor", None),
        P("dp"),
    )
    return jax.shard_map(
        shards,
        mesh=mesh,
        in_specs=placed,
        out_specs=(
            P(("blk", "tensor"), "dp", None),
            P(("blk", "tensor"), "dp", None),
            P(None, None, "tensor"),
            P("tensor", None),
            P(None, None, "tensor"),
            P("tensor", None),
            P(),
            P(),
        ),
        check_vma=False,
    )
```

```python
import functools
import math

import jax
import jax.numpy as jnp
from jax import lax
from jax.experimental import pallas as pl
from jax.experimental.pallas import tpu as pltpu
from jax.sharding import PartitionSpec as P

HD = 64
EPSILON = 1e-05
MASKED = -1000000000.0
F32 = jnp.float32
BF16 = jnp.bfloat16
MIB = 1024 * 1024
FFN_ORDER = (1, 3, 2, 0)


def send_y(values, step):
    pairs = [(i, ((i // 2 + step) % 4) * 2 + i % 2) for i in range(8)]
    return lax.ppermute(values, "tensor", pairs)


def send_pair(values):
    return lax.ppermute(values, "tensor", [(i, i ^ 1) for i in range(8)])


def send_z(values, step):
    return lax.ppermute(values, "blk", [(i, (i + step) % 4) for i in range(4)])


def send_core(values):
    return lax.ppermute(values, "dp", [(i, i ^ 1) for i in range(4)])


def send_far(values):
    return lax.ppermute(values, "dp", [(i, i ^ 2) for i in range(4)])


def send_x(values, steps):
    pairs = []
    for d in range(4):
        for t in range(8):
            core = d % 2
            x = ((d // 2) * 2 + t % 2 + steps[core]) % 4
            pairs.append((d * 8 + t, ((x // 2) * 2 + core) * 8 + (t // 2) * 2 + x % 2))
    return lax.ppermute(values, ("dp", "tensor"), pairs)


def gather_y(values):
    return [values] + [send_y(values, -r) for r in (1, 2, 3)]


def scatter_y(parts):
    return [parts[0]] + [send_y(parts[r], r) for r in (1, 2, 3)]


def gather_z(parts):
    return [parts[0]] + [send_z(parts[r], r) for r in (1, 2, 3)]


def scatter_z(parts):
    return [parts[0]] + [send_z(parts[r], -r) for r in (1, 2, 3)]


def norm_parts(values):
    mean = jnp.mean(values, axis=-1, keepdims=True)
    centred = values - mean
    inverse = lax.rsqrt(jnp.mean(centred * centred, axis=-1, keepdims=True) + EPSILON)
    return centred * inverse, inverse


def norm_back(normed, inverse, gain, cotangent):
    e = cotangent * gain
    grad = (
        e
        - jnp.mean(e, axis=-1, keepdims=True)
        - normed * jnp.mean(e * normed, axis=-1, keepdims=True)
    ) * inverse
    return grad, jnp.sum(cotangent * normed, axis=0), jnp.sum(cotangent, axis=0)


def dot(a, b, ca, cb):
    return lax.dot_general(a, b, (((ca,), (cb,)), ((), ())), preferred_element_type=F32)


def rows_of(refs):
    return jnp.concatenate([r[...] for r in refs], axis=0)


def put_rows(refs, values):
    rows = refs[0].shape[0]
    for i, ref in enumerate(refs):
        ref[...] = values[i * rows : (i + 1) * rows].astype(ref.dtype)


def call(kernel, name, inputs, outs, flops, after=(), mib=8, micros=4):
    count = len(inputs)
    entries = [v[1] if isinstance(v, tuple) else None for v in inputs]
    inputs = [v[0] if isinstance(v, tuple) else v for v in inputs]

    def body(*refs):
        ins = [r if i is None else r.at[i] for r, i in zip(refs, entries)]
        kernel(ins, refs[count + len(after) :])

    return pl.pallas_call(
        body,
        in_specs=[
            pl.BlockSpec(memory_space=pltpu.SMEM if v.dtype == jnp.int32 else pltpu.VMEM)
            for v in inputs
        ]
        + [pl.BlockSpec(memory_space=pl.ANY)] * len(after),
        out_specs=[pl.BlockSpec(memory_space=pltpu.VMEM)] * len(outs),
        out_shape=[jax.ShapeDtypeStruct(shape, dtype) for shape, dtype in outs],
        compiler_params=pltpu.CompilerParams(vmem_limit_bytes=mib * MIB),
        cost_estimate=pl.CostEstimate(flops=6 * flops + micros * 1_000_000_000, bytes_accessed=4_000_000, transcendentals=0),
        name=name,
    )(*inputs, *after)


def heads_prepare_kernel(ins, outs):
    w_qkv, w_out, core = ins
    for part in range(3):
        turned = w_qkv[part].T
        for j in range(2):
            outs[0][j, part * HD : (part + 1) * HD] = turned[j * HD : (j + 1) * HD]
    for j in range(2):
        outs[0][j, 3 * HD :] = w_out[j * HD : (j + 1) * HD]
    outs[1][...] = outs[0][core[0]]


def heads_order_kernel(ins, outs):
    own, recv, other, places = ins
    for r in range(4):
        place = places[r]
        head = jnp.where(place < 2, own[jnp.minimum(place, 1)], jnp.where(place == 2, recv[...], other[...]))
        outs[0][3 * HD * r : 3 * HD * (r + 1)] = head[: 3 * HD]
        outs[1][HD * r : HD * (r + 1)] = head[3 * HD :]


def units_prepare_kernel(ins, outs):
    w_gate_up, w_down, core = ins
    half = w_down.shape[0] // 2
    for j in range(2):
        for part in range(2):
            outs[0][j, part] = w_gate_up[part, :, j * half : (j + 1) * half].T
        outs[0][j, 2] = w_down[j * half : (j + 1) * half]
    outs[1][...] = outs[0][core[0]]


def total(refs):
    return sum(r[...].astype(F32) for r in refs)


def window_rows(refs, j, rows):
    return jnp.concatenate([r[j * rows : (j + 1) * rows] for r in refs], axis=0)


def put_window_parts(refs, products):
    rows = products[0].shape[0] // 4
    for r, ref in enumerate(refs):
        for j, product in enumerate(products):
            ref[j * rows : (j + 1) * rows] = product[r * rows : (r + 1) * rows].astype(ref.dtype)


def project_kernel(windows, ins, outs):
    w_in, gain, offset, cosine, sine = ins[4:9]
    rows = outs[0].shape[2] // 4
    c, s = cosine[...], sine[...]
    half = HD // 2
    for j, window in enumerate(windows):
        normed, _ = norm_parts(window_rows(ins[:4], window, rows).astype(F32))
        outs[4][j] = normed.astype(BF16)
        h1 = (normed * gain[...] + offset[...]).astype(BF16)
        proj = dot(w_in[...], h1, 1, 1)
        for r in range(4):
            for part in range(3):
                at = (3 * r + part) * HD
                first, second = proj[at : at + half], proj[at + half : at + HD]
                if part < 2:
                    first, second = first * c - second * s, second * c + first * s
                if part == 0:
                    first, second = first * 0.125, second * 0.125
                outs[r][j, part * HD : part * HD + half, :] = first.astype(BF16)
                outs[r][j, part * HD + half : (part + 1) * HD, :] = second.astype(BF16)


def stack_kernel(ins, outs):
    for r in range(4):
        outs[0][r] = ins[r][HD:, :]


def join_kernel(ins, outs):
    for j in range(outs[0].shape[0]):
        outs[0][j] = jnp.concatenate([r[j] for r in ins], axis=0)


def out_kernel(ins, outs):
    ob = [ins[0][j] for j in range(ins[0].shape[0])] + [rows_of(ins[1:5])]
    outs[4][...] = ob[-1]
    put_window_parts(outs[:4], [dot(v.T, ins[5][...], 1, 0) for v in ob])


def middle_kernel(ins, outs):
    middle = total(ins[:5])
    normed, _ = norm_parts(middle)
    outs[0][...] = middle
    outs[1][...] = (normed * ins[5][...] + ins[6][...]).astype(BF16)


def middle_back_kernel(ins, outs):
    dh2 = ins[0][...] + ins[1][...].astype(F32)
    normed, inv = norm_parts(ins[2][...])
    back, g_scale, g_shift = norm_back(normed, inv, ins[4][...], dh2)
    dx2 = ins[3][...].astype(F32) + back
    outs[0][...] = dx2
    outs[1][...] = dx2.astype(BF16)
    outs[2][...] = jnp.concatenate([g_scale[None], g_shift[None]], axis=0)


def out_back_kernel(windows, ins, outs):
    for j, window in enumerate(windows):
        da = window_rows(ins[:4], window, outs[0].shape[2] // 4)
        outs[4][j] = da
        dob = dot(ins[4][...], da, 1, 1)
        for r in range(4):
            outs[r][j] = dob[r * HD : (r + 1) * HD].astype(BF16)


def merge_kernel(ins, outs):
    for j in range(outs[0].shape[0]):
        own, pair = ins[5 * j : 5 * j + 4], ins[5 * j + 4]
        for r in range(4):
            outs[r][j, :HD, :] = own[r][:HD, :]
            outs[r][j, HD:, :] = (own[r][HD:, :].astype(F32) + pair[r].astype(F32)).astype(BF16)


def project_back_kernel(ins, outs):
    w_in, cosine, sine = ins[4:7]
    c, s = cosine[...], sine[...]
    half = HD // 2
    pieces = []
    for r in range(4):
        for part in range(2):
            first = ins[r][part * HD : part * HD + half, :].astype(F32)
            second = ins[r][part * HD + half : (part + 1) * HD, :].astype(F32)
            pieces.append((first * c + second * s).astype(BF16))
            pieces.append((second * c - first * s).astype(BF16))
        pieces.append(ins[r][2 * HD :, :])
    d_proj = jnp.concatenate(pieces, axis=0)
    outs[0][...] = d_proj
    product = dot(d_proj.T, w_in[...], 1, 0)
    if len(outs) == 2:
        outs[1][...] = product.astype(BF16)
    else:
        put_window_parts(outs[1:], [r[...] for r in ins[7:]] + [product])


def input_back_kernel(ins, outs):
    dh1 = total(ins[:2])
    normed, inv = norm_parts(ins[2][...].astype(F32))
    back, _, _ = norm_back(normed, inv, ins[4][...], dh1)
    outs[0][...] = (ins[3][...] + back).astype(BF16)


def heads_kernel(ins, outs):
    back, w_in, gain, offset, slots, second = ins[:6]
    products, sums = 0.0, 0.0
    for d_proj, normed in zip(ins[6:9], ins[9:12]):
        products = products + dot(d_proj[...], normed[...], 1, 0)
        sums = sums + jnp.sum(d_proj[...].astype(F32), axis=1, keepdims=True)
    g_in = (products * gain[...] + sums * offset[...]).astype(BF16)
    wide = w_in[...].astype(F32)
    small = [
        jnp.sum(wide * products, axis=0, keepdims=True),
        second[:1, :],
        jnp.sum(wide * sums, axis=0, keepdims=True),
        second[1:, :],
    ]
    row = lax.broadcasted_iota(jnp.int32, (16, g_in.shape[1]), 0)
    small = [jnp.where(row == 0, v, 0.0).astype(BF16) for v in small]

    def put(out, slot, r):
        for chunk in range(4):
            if chunk < 3:
                rows = g_in[3 * HD * r + HD * chunk : 3 * HD * r + HD * (chunk + 1)]
            else:
                rows = back[HD * r : HD * (r + 1)].astype(BF16)
            out[slot, chunk, :HD] = rows
            out[slot, chunk, HD:] = small[chunk]

    for r in range(4):
        slot = slots[r]

        @pl.when(slot < 2)
        def _(slot=slot, r=r):
            put(outs[0], slot, r)

        @pl.when(slot >= 2)
        def _(slot=slot, r=r):
            put(outs[1], slot - 2, r)


def heads_core_kernel(ins, outs):
    for i in range(2):
        outs[i][...] = (ins[0][i].astype(F32) + ins[1][i].astype(F32)).astype(BF16)


def heads_pair_kernel(ins, outs):
    for r in range(4):
        chunk = lax.rem(ins[2][0] + r, 4)
        outs[r][...] = (ins[0][chunk].astype(F32) + ins[1][chunk].astype(F32)).astype(BF16)


def sum_kernel(ins, outs):
    outs[0][...] = total(ins).astype(outs[0].dtype)


def heads_ring_kernel(ins, outs):
    for r in range(4):
        chunk = lax.rem(ins[4][0] + r, 4)
        outs[0][chunk] = ins[r][...]
    for r in range(4):
        outs[1][lax.rem(ins[4][0] + r, 4)] = ins[r][HD : HD + 1].astype(F32)


def out_grad_kernel(ins, outs):
    outs[0][...] = sum(dot(ob[...], da[...], 1, 0) for ob, da in zip(ins[:3], ins[3:]))


def by_core(core, mine, other):
    low = jnp.where(core == 0, mine, other).astype(F32)
    high = jnp.where(core == 0, other, mine).astype(F32)
    return low, high


def units_final_kernel(ins, outs):
    low, high = by_core(ins[2][0], ins[0][...], ins[1][...])
    half = low.shape[0] // 3
    for side, values in enumerate((low, high)):
        for part in range(2):
            outs[0][part, :, side * half : (side + 1) * half] = values[
                part * half : (part + 1) * half
            ].T
        outs[1][side * half : (side + 1) * half] = values[2 * half :]


def heads_final_kernel(ins, outs):
    low, high = by_core(ins[2][0], ins[0][:, :HD], ins[1][:, :HD])
    for part in range(3):
        outs[0][part] = jnp.concatenate([low[part], high[part]], axis=0).T
    outs[1][...] = jnp.concatenate([low[3], high[3]], axis=0)


def halves_kernel(ins, outs):
    half = outs[0].shape[0]
    outs[0][...] = ins[0][:half]
    outs[1][...] = ins[1][half:]


def touch_kernel(ins, outs):
    outs[0][...] = jnp.zeros_like(outs[0])


def copy_kernel(ins, outs):
    for ref, out in zip(ins, outs):
        out[...] = ref[...]


def result_kernel(ins, outs):
    outs[0][...] = total(ins).astype(BF16)


def ffn_kernel(r, ins, outs):
    dy_in, own, recv, other, y = ins[-5:]
    dh2_out, y_out, hid_out, d_gu_out = outs[:4]
    h2 = rows_of(ins[:-5])
    dy = dy_in[lax.rem(y[0] + r, 4)]
    acc_dh2, acc_y = 0.0, 0.0
    for i, (w_gate, w_up, w_down) in enumerate(
        [[own[j, part] for part in range(3)] for j in range(2)]
        + [[ref[part] for part in range(3)] for ref in (recv, other)]
    ):
        gate = dot(h2, w_gate, 1, 1)
        up = dot(h2, w_up, 1, 1)
        dh = dot(dy, w_down, 1, 1)
        sig = 1.0 / (1.0 + jnp.exp(-gate))
        act = gate * sig
        hid = (act * up).astype(BF16)
        d_gate = (dh * up * (sig + act * (1.0 - sig))).astype(BF16)
        d_up = (dh * act).astype(BF16)
        hid_out[i] = hid
        d_gu_out[i, 0] = d_gate
        d_gu_out[i, 1] = d_up
        acc_dh2 = acc_dh2 + dot(d_gate, w_gate, 1, 0) + dot(d_up, w_up, 1, 0)
        acc_y = acc_y + dot(hid, w_down, 1, 0)
    dh2_out[...] = acc_dh2.astype(BF16)
    y_out[...] = acc_y.astype(BF16)


def ffn_grad_kernel(ins, outs):
    hid, d_gu, dy, flags = ins[:4], ins[4:8], ins[13], ins[14]
    h2_all = rows_of(ins[8:13])
    core, y = flags[0], flags[1]
    dy_all = jnp.concatenate([dy[lax.rem(y + r, 4)] for r in range(4)], axis=0)
    for out, slot, block in ((1, 0, 1 - core), (1, 1, 3), (0, 0, core), (0, 1, 2)):
        for part in range(2):
            d_block = jnp.concatenate([r[block, part] for r in d_gu], axis=0)
            outs[out][slot, part] = dot(d_block.T, h2_all, 1, 0).astype(BF16)
        hid_block = jnp.concatenate([r[block] for r in hid], axis=0)
        outs[out][slot, 2] = dot(hid_block.T, dy_all, 1, 0).astype(BF16)


def load_keys(own, pair, places):
    keys = jnp.concatenate([r[HD : 2 * HD, :] for r in own] + [pair[i, :HD] for i in range(4)], axis=1)
    values = jnp.concatenate([r[2 * HD :, :] for r in own] + [pair[i, HD:] for i in range(4)], axis=1)
    z, y, xl = places[0], places[1], places[2]
    tokens = own[0].shape[1]
    rows = tokens // 4
    lane = lax.broadcasted_iota(jnp.int32, (1, 8 * tokens), 1)
    source, within = lane // tokens, lane % tokens
    side = jnp.where(source < 4, xl, 1 - xl)
    at = ((z + 4 - source % 4) % 4) * (8 * rows) + ((y + within // rows) % 4) * (2 * rows)
    at = at + side * rows + within % rows
    bias = jnp.where(at < places[3], 0.0, MASKED)
    row = lax.broadcasted_iota(jnp.int32, (16, 8 * tokens), 0)
    extra = jnp.where(row == 0, bias, 0.0).astype(BF16)
    return keys, values, jnp.concatenate([keys, extra], axis=0)


def with_one(queries):
    row = lax.broadcasted_iota(jnp.int32, (16, queries.shape[1]), 0)
    return jnp.concatenate([queries, jnp.where(row == 0, 1.0, 0.0).astype(BF16)], axis=0)


def attend_kernel(ins, outs):
    own, pair, places, before = ins[0:4], ins[4], ins[5], ins[6:]
    out, wide, lse = outs[0:4], outs[4], outs[5]
    _, values, keys_bias = load_keys(own, pair, places)
    keys_rows = keys_bias.T
    for i in range(4):
        scores = dot(keys_rows, with_one(own[i][:HD, :]), 1, 0)
        top = jnp.max(scores, axis=0, keepdims=True)
        weights = jnp.exp(scores - top)
        total = jnp.sum(weights, axis=0, keepdims=True)
        attended = dot(values, weights.astype(BF16), 1, 0) * (1.0 / total)
        wide[i] = attended
        if before:
            out[i][0] = before[i][...]
            out[i][1] = attended.astype(BF16)
        else:
            out[i][...] = attended.astype(BF16)
        lse[i] = top + jnp.log(total)


def attend_back_kernel(ins, outs):
    own, pair, places = ins[0:4], ins[4], ins[5]
    dob, wide, lse = ins[6:10], ins[10], ins[11]
    d_own, d_pair = outs[0:4], outs[4]
    width = own[0].shape[1]
    keys, values, keys_bias = load_keys(own, pair, places)
    keys_rows = keys_bias.T
    values_rows = values.T
    dk = jnp.zeros((keys.shape[1], HD), F32)
    dv = jnp.zeros((keys.shape[1], HD), F32)
    for i in range(4):
        queries, grad = own[i][:HD, :], dob[i][...]
        scores = dot(keys_rows, with_one(queries), 1, 0)
        weights = jnp.exp(scores - lse[i])
        delta = jnp.sum(grad.astype(F32) * wide[i], axis=0, keepdims=True)
        grad_weights = dot(values_rows, grad, 1, 0)
        grad_scores = (weights * (grad_weights - delta)).astype(BF16)
        d_own[i][:HD, :] = (dot(keys, grad_scores, 1, 0) * 0.125).astype(BF16)
        dk = dk + dot(grad_scores, queries, 1, 1)
        dv = dv + dot(weights.astype(BF16), grad, 1, 1)
    dkv = jnp.concatenate([dk, dv], axis=1).T
    for i in range(4):
        d_own[i][HD:, :] = dkv[:, i * width : (i + 1) * width].astype(BF16)
        d_pair[i] = dkv[:, (4 + i) * width : (5 + i) * width].astype(BF16)


Y_GROUPS = [[0, 2, 4, 6], [1, 3, 5, 7]]


def shards(hidden_in, out_grad, norm_scales, norm_shifts, w_qkv, w_out, w_gate_up, w_down, lengths):
    rows, windows, width = hidden_in.shape
    tensor = lax.axis_index("tensor")
    y, xl = tensor // 2, tensor % 2
    z = lax.axis_index("blk")
    core = lax.axis_index("dp") % 2
    tokens = 4 * rows
    ff = w_down.shape[0]
    half = ff // 2

    order = []

    x_rows = hidden_in.transpose(1, 0, 2).reshape(windows * rows, width)
    dy_rows = out_grad.transpose(1, 0, 2).reshape(windows * rows, width)
    x_all = gather_y(x_rows)
    dy_abs = lax.all_gather(dy_rows, "tensor", axis=0, axis_index_groups=Y_GROUPS)

    y_index = jnp.full((1,), y, jnp.int32)
    z_index = jnp.full((1,), z, jnp.int32)
    flag = jnp.full((1,), core, jnp.int32)
    core_y = jnp.stack([core, y]).astype(jnp.int32)
    heads_at = (z + jnp.arange(4, dtype=jnp.int32)) % 4
    slots = jnp.where(heads_at // 2 == xl, 0, 1) + jnp.where(heads_at % 2 == core, 0, 2)
    places = jnp.where(heads_at // 2 == xl, heads_at % 2, 2 + ((heads_at % 2) ^ core))
    here = [jnp.stack([z, y, xl, lengths[w]]).astype(jnp.int32) for w in range(windows)]

    heads_own, heads_recv = call(
        heads_prepare_kernel, "heads_prepare", [w_qkv, w_out, flag],
        [((2, 4 * HD, width), BF16), ((4 * HD, width), BF16)], 0,
    )
    heads_recv = send_x(heads_recv, (-1, 1))
    units_own, units_recv = call(
        units_prepare_kernel, "units_prepare", [w_gate_up, w_down, flag],
        [((2, 3, half, width), BF16), ((3, half, width), BF16)], 0, [heads_own], 12,
    )
    w_in, w_back = call(
        heads_order_kernel, "heads_order", [heads_own, heads_recv, send_core(heads_recv), places],
        [((12 * HD, width), BF16), ((4 * HD, width), BF16)], 0, [units_own],
    )
    units_recv = send_x(units_recv, (-1, 1))
    units_other = send_core(units_recv)

    lane = jnp.arange(tokens, dtype=jnp.int32)
    within = ((y + lane // rows) % 4) * (2 * rows) + lane % rows
    inverse = 10000.0 ** (-(jnp.arange(HD // 2, dtype=F32) * 2.0) / HD)
    angles = inverse[:, None] * (z * (8 * rows) + within + xl * rows).astype(F32)[None, :]
    cosine, sine = jnp.cos(angles), jnp.sin(angles)

    gain = [norm_scales[i : i + 1] for i in range(2)]
    offset = [norm_shifts[i : i + 1] for i in range(2)]
    work = 2 * tokens * width * tokens
    piece, piece_wide = ((windows * rows, width), BF16), ((windows * rows, width), F32)
    head_piece, triple = ((HD, tokens), BF16), ((3 * HD, tokens), BF16)
    each = range(windows)

    def after(value):
        order.append(value)

    def last():
        return order[-1:]

    def add_core(kept, given, deps):
        shape = (kept.shape[1:], BF16)
        own, far = call(heads_core_kernel, "add_core", [kept, given], [shape] * 2, 0, deps)
        after(own)
        return own, far

    def run(kernel, name, inputs, outs, flops=0, mib=8, micros=4):
        out = call(kernel, name, inputs, outs, flops, last(), mib, micros)
        after(out[0])
        return out

    own, pair, wide, lse = ([None] * windows for _ in range(4))

    def entries(arrays, i):
        return [(v, i) for v in arrays]

    def project(*group):
        *sent, normed = run(
            functools.partial(project_kernel, group), "project",
            [*x_all, w_in, gain[0], offset[0], cosine, sine],
            [((len(group), 3 * HD, tokens), BF16)] * 4 + [((len(group), tokens, width), BF16)],
            3 * len(group) * work, 10,
        )
        sent = gather_z(sent)
        for i, w in enumerate(group):
            own[w] = entries(sent, i)
        return normed

    def stack(w):
        (pair[w],) = run(stack_kernel, "stack", own[w], [((4, 2 * HD, tokens), BF16)])
        pair[w] = send_pair(pair[w])

    def attend(w, before=()):
        *parts, wide[w], lse[w] = run(
            attend_kernel, "attend", [*own[w], pair[w], here[w], *before],
            [((2, HD, tokens) if before else (HD, tokens), BF16)] * 4
            + [((4, HD, tokens), F32), ((4, 1, tokens), F32)],
            128 * HD * tokens * tokens, 10,
        )
        return parts

    normed_all = [project(0), project(1, 2)]
    stack(0)
    stack(1)
    out = attend(0)
    stack(2)
    out = scatter_z(attend(1, out))
    out_last = scatter_z(attend(2))
    (ob,) = run(join_kernel, "join", out, [((2, 4 * HD, tokens), BF16)])
    *parts, ob_last = run(
        out_kernel, "out_project", [ob, *out_last, w_back],
        [piece] * 4 + [((4 * HD, tokens), BF16)], 3 * work,
    )
    middle, h2 = run(
        middle_kernel, "middle", [*scatter_y(parts), x_rows, gain[1], offset[1]], [piece_wide, piece]
    )

    h2_after, h2_before = send_y(h2, -1), send_y(h2, 1)
    run(touch_kernel, "touch", [dy_abs, units_own, units_recv, units_other], [((8, 128), F32)])
    near = run(halves_kernel, "halves", [h2_after, h2_before], [((windows * rows // 2, width), BF16)] * 2)
    h2_all = [h2, h2_after, [send_y(near[0], -1), send_y(near[1], 1)], h2_before]
    dh2, y_part, hid, d_gu = [None] * 4, [None] * 4, [None] * 4, [None] * 4
    for r in FFN_ORDER:
        dh2[r], y_part[r], hid[r], d_gu[r] = run(
            functools.partial(ffn_kernel, r), "ffn",
            [*(h2_all[r] if r == 2 else h2_all[r : r + 1]), dy_abs, units_own, units_recv, units_other, y_index],
            [piece, piece, ((4, windows * rows, half), BF16), ((4, 2, windows * rows, half), BF16)],
            18 * work, 10,
        )
        if r:
            dh2[r] = send_y(dh2[r], r)
    (dh2_near,) = run(sum_kernel, "add", [dh2[0], dh2[1], dh2[3]], [piece_wide])
    units, units_given = run(
        ffn_grad_kernel, "ffn_grad", [*hid, *d_gu, *h2_all[:2], *h2_all[2], h2_before, dy_abs, core_y],
        [((2, 3, half, width), BF16)] * 2, 36 * work, 10,
    )
    units_given = send_core(units_given)
    dx2, da, norm_sums = run(
        middle_back_kernel, "middle_back", [dh2_near, dh2[2], middle, dy_rows, gain[1]],
        [piece_wide, piece, ((2, width), F32)],
    )
    da_all = gather_y(da)

    def out_back(*group):
        *parts, rows_all = run(
            functools.partial(out_back_kernel, group), "out_back", [*da_all, w_back],
            [((len(group), HD, tokens), BF16)] * 4 + [((len(group), tokens, width), BF16)],
            len(group) * work, micros=20,
        )
        return gather_z(parts), rows_all

    def attend_back(w, dob):
        *d_own, d_pair = run(
            attend_back_kernel, "attend_back",
            [*own[w], pair[w], here[w], *dob, wide[w], lse[w]],
            [triple] * 4 + [((4, 2 * HD, tokens), BF16)], 320 * HD * tokens * tokens, 14,
        )
        return d_own, send_pair(d_pair)

    def merge(*parts):
        return scatter_z(
            run(
                merge_kernel, "merge", [v for d_own, d_pair in parts for v in (*d_own, d_pair)],
                [((len(parts), 3 * HD, tokens), BF16)] * 4,
            )
        )

    dob, da_rows = out_back(0)
    dob_rest, da_rest = out_back(1, 2)
    units, units_far = add_core(units, units_given, last())
    units_far = send_x(units_far, (-1, 1))
    y_part = scatter_y(run(copy_kernel, "copy", y_part, [piece] * 4))
    d_first = attend_back(0, entries(dob, 0))
    d_second = attend_back(1, entries(dob_rest, 0))
    (units,) = run(sum_kernel, "add", [units, units_far], [(units.shape, BF16)])
    units = lax.psum_scatter(units.reshape(-1, width), "blk", scatter_dimension=0, tiled=True)
    def project_back(d_sent, earlier=(), last_one=False):
        return run(
            project_back_kernel, "project_back", [*entries(d_sent, 0), w_in, cosine, sine, *earlier],
            [((12 * HD, tokens), BF16)] + ([piece] * 4 if last_one else [((tokens, width), BF16)]),
            3 * work,
        )

    d_first = merge(d_first)
    d_third = attend_back(2, entries(dob_rest, 1))
    d_second = merge(d_second)
    d_proj = [None] * windows
    d_proj[0], product_first = project_back(d_first)
    (g_back,) = run(
        out_grad_kernel, "out_grads", [(ob, 0), (ob, 1), ob_last, (da_rows, 0), (da_rest, 0), (da_rest, 1)],
        [((4 * HD, width), F32)], 3 * work,
    )
    d_third = merge(d_third)
    d_proj[1], product_second = project_back(d_second)
    (result,) = run(result_kernel, "result", [*y_part, middle], [piece])
    (units,) = run(sum_kernel, "add", [units, send_far(units)], [(units.shape, BF16)])
    units = lax.all_gather(units, "blk", axis=0, tiled=True)
    d_proj[2], *parts = project_back(d_third, [product_first, product_second], True)
    dh1 = scatter_y(parts)
    wide_heads = ((2, 4, HD + 16, width), BF16)
    heads, heads_given = run(
        heads_kernel, "heads",
        [g_back, w_in, gain[0], offset[0], slots, norm_sums, *d_proj]
        + [(normed_all[0], 0), (normed_all[1], 0), (normed_all[1], 1)],
        [wide_heads, wide_heads], 9 * work, 10,
    )
    heads, heads_far = add_core(heads, send_core(heads_given), last())
    heads_far = send_x(heads_far, (-1, 1))
    (dh1_near,) = run(sum_kernel, "add", [dh1[0], dh1[1], dh1[3]], [piece_wide])
    chunk = ((HD + 16, width), BF16)
    parts = run(heads_pair_kernel, "add_pair", [heads, heads_far, z_index], [chunk] * 4)
    parts = [parts[0]] + [send_z(parts[r], r) for r in (1, 2, 3)]
    (part,) = run(sum_kernel, "add", parts, [chunk])
    (part,) = run(sum_kernel, "add", [part, send_far(part)], [chunk])
    (grad_in,) = run(
        input_back_kernel, "input_back", [dh1_near, dh1[2], x_rows, dx2, gain[0]], [piece]
    )
    ring = [part] + [send_z(part, -r) for r in (1, 2, 3)]
    grad_gate_up, grad_down = run(
        units_final_kernel, "units_final", [units, send_core(units), flag],
        [((2, width, ff), F32), ((ff, width), F32)],
    )
    heads, small = run(
        heads_ring_kernel, "ring", [*ring, z_index],
        [((4, HD + 16, width), BF16), ((4, 1, width), F32)],
    )
    grad_qkv, grad_out = run(
        heads_final_kernel, "heads_final", [heads, send_core(heads), flag],
        [((3, width, 2 * HD), F32), ((2 * HD, width), F32)],
    )
    small = small.reshape(4, width)
    small = small + sum(send_y(small, r) for r in (1, 2, 3))

    return (
        result.reshape(windows, rows, width).transpose(1, 0, 2),
        grad_in.reshape(windows, rows, width).transpose(1, 0, 2),
        grad_qkv,
        grad_out,
        grad_gate_up,
        grad_down,
        small[:2],
        small[2:],
    )


def solution(mesh):
    placed = (
        P(("blk", "tensor"), "dp", None),
        P(("blk", "tensor"), "dp", None),
        P(),
        P(),
        P(None, None, "tensor"),
        P("tensor", None),
        P(None, None, "tensor"),
        P("tensor", None),
        P("dp"),
    )
    return jax.shard_map(
        shards,
        mesh=mesh,
        in_specs=placed,
        out_specs=(
            P(("blk", "tensor"), "dp", None),
            P(("blk", "tensor"), "dp", None),
            P(None, None, "tensor"),
            P("tensor", None),
            P(None, None, "tensor"),
            P("tensor", None),
            P(),
            P(),
        ),
        check_vma=False,
    )
```

```python
import functools
import math

import jax
import jax.numpy as jnp
from jax import lax
from jax.experimental import pallas as pl
from jax.experimental.pallas import tpu as pltpu
from jax.sharding import PartitionSpec as P

HD = 64
EPSILON = 1e-05
MASKED = -1000000000.0
F32 = jnp.float32
BF16 = jnp.bfloat16
MIB = 1024 * 1024
FFN_ORDER = (1, 3, 2, 0)


def send_y(values, step):
    pairs = [(i, ((i // 2 + step) % 4) * 2 + i % 2) for i in range(8)]
    return lax.ppermute(values, "tensor", pairs)


def send_pair(values):
    return lax.ppermute(values, "tensor", [(i, i ^ 1) for i in range(8)])


def send_z(values, step):
    return lax.ppermute(values, "blk", [(i, (i + step) % 4) for i in range(4)])


def send_core(values):
    return lax.ppermute(values, "dp", [(i, i ^ 1) for i in range(4)])


def send_far(values):
    return lax.ppermute(values, "dp", [(i, i ^ 2) for i in range(4)])


def send_x(values, steps):
    pairs = []
    for d in range(4):
        for t in range(8):
            core = d % 2
            x = ((d // 2) * 2 + t % 2 + steps[core]) % 4
            pairs.append((d * 8 + t, ((x // 2) * 2 + core) * 8 + (t // 2) * 2 + x % 2))
    return lax.ppermute(values, ("dp", "tensor"), pairs)


def gather_y(values):
    return [values] + [send_y(values, -r) for r in (1, 2, 3)]


def scatter_y(parts):
    return [parts[0]] + [send_y(parts[r], r) for r in (1, 2, 3)]


def gather_z(parts):
    return [parts[0]] + [send_z(parts[r], r) for r in (1, 2, 3)]


def scatter_z(parts):
    return [parts[0]] + [send_z(parts[r], -r) for r in (1, 2, 3)]


def norm_parts(values):
    mean = jnp.mean(values, axis=-1, keepdims=True)
    centred = values - mean
    inverse = lax.rsqrt(jnp.mean(centred * centred, axis=-1, keepdims=True) + EPSILON)
    return centred * inverse, inverse


def norm_back(normed, inverse, gain, cotangent):
    e = cotangent * gain
    grad = (
        e
        - jnp.mean(e, axis=-1, keepdims=True)
        - normed * jnp.mean(e * normed, axis=-1, keepdims=True)
    ) * inverse
    return grad, jnp.sum(cotangent * normed, axis=0), jnp.sum(cotangent, axis=0)


def dot(a, b, ca, cb):
    return lax.dot_general(a, b, (((ca,), (cb,)), ((), ())), preferred_element_type=F32)


def rows_of(refs):
    return jnp.concatenate([r[...] for r in refs], axis=0)


def put_rows(refs, values):
    rows = refs[0].shape[0]
    for i, ref in enumerate(refs):
        ref[...] = values[i * rows : (i + 1) * rows].astype(ref.dtype)


def call(kernel, name, inputs, outs, flops, after=(), mib=8, micros=4):
    count = len(inputs)
    entries = [v[1] if isinstance(v, tuple) else None for v in inputs]
    inputs = [v[0] if isinstance(v, tuple) else v for v in inputs]

    def body(*refs):
        ins = [r if i is None else r.at[i] for r, i in zip(refs, entries)]
        kernel(ins, refs[count + len(after) :])

    return pl.pallas_call(
        body,
        in_specs=[
            pl.BlockSpec(memory_space=pltpu.SMEM if v.dtype == jnp.int32 else pltpu.VMEM)
            for v in inputs
        ]
        + [pl.BlockSpec(memory_space=pl.ANY)] * len(after),
        out_specs=[pl.BlockSpec(memory_space=pltpu.VMEM)] * len(outs),
        out_shape=[jax.ShapeDtypeStruct(shape, dtype) for shape, dtype in outs],
        compiler_params=pltpu.CompilerParams(vmem_limit_bytes=mib * MIB),
        cost_estimate=pl.CostEstimate(flops=6 * flops + micros * 1_000_000_000, bytes_accessed=4_000_000, transcendentals=0),
        name=name,
    )(*inputs, *after)


def heads_prepare_kernel(ins, outs):
    w_qkv, w_out, core = ins
    for part in range(3):
        turned = w_qkv[part].T
        for j in range(2):
            outs[0][j, part * HD : (part + 1) * HD] = turned[j * HD : (j + 1) * HD]
    for j in range(2):
        outs[0][j, 3 * HD :] = w_out[j * HD : (j + 1) * HD]
    outs[1][...] = outs[0][core[0]]


def heads_order_kernel(ins, outs):
    own, recv, other, places = ins
    for r in range(4):
        place = places[r]
        head = jnp.where(place < 2, own[jnp.minimum(place, 1)], jnp.where(place == 2, recv[...], other[...]))
        outs[0][3 * HD * r : 3 * HD * (r + 1)] = head[: 3 * HD]
        outs[1][HD * r : HD * (r + 1)] = head[3 * HD :]


def units_prepare_kernel(ins, outs):
    w_gate_up, w_down, core = ins
    half = w_down.shape[0] // 2
    for j in range(2):
        for part in range(2):
            outs[0][j, part] = w_gate_up[part, :, j * half : (j + 1) * half].T
        outs[0][j, 2] = w_down[j * half : (j + 1) * half]
    outs[1][...] = outs[0][core[0]]


def total(refs):
    return sum(r[...].astype(F32) for r in refs)


def window_rows(refs, j, rows):
    return jnp.concatenate([r[j * rows : (j + 1) * rows] for r in refs], axis=0)


def put_window_parts(refs, products):
    rows = products[0].shape[0] // 4
    for r, ref in enumerate(refs):
        for j, product in enumerate(products):
            ref[j * rows : (j + 1) * rows] = product[r * rows : (r + 1) * rows].astype(ref.dtype)


def project_kernel(windows, ins, outs):
    w_in, gain, offset, cosine, sine = ins[4:9]
    rows = outs[0].shape[2] // 4
    c, s = cosine[...], sine[...]
    half = HD // 2
    for j, window in enumerate(windows):
        normed, _ = norm_parts(window_rows(ins[:4], window, rows).astype(F32))
        outs[4][j] = normed.astype(BF16)
        h1 = (normed * gain[...] + offset[...]).astype(BF16)
        proj = dot(w_in[...], h1, 1, 1)
        for r in range(4):
            for part in range(3):
                at = (3 * r + part) * HD
                first, second = proj[at : at + half], proj[at + half : at + HD]
                if part < 2:
                    first, second = first * c - second * s, second * c + first * s
                if part == 0:
                    first, second = first * 0.125, second * 0.125
                outs[r][j, part * HD : part * HD + half, :] = first.astype(BF16)
                outs[r][j, part * HD + half : (part + 1) * HD, :] = second.astype(BF16)


def stack_kernel(ins, outs):
    for r in range(4):
        outs[0][r] = ins[r][HD:, :]


def join_kernel(ins, outs):
    for j in range(outs[0].shape[0]):
        outs[0][j] = jnp.concatenate([r[j] for r in ins], axis=0)


def out_kernel(ins, outs):
    ob = [ins[0][j] for j in range(ins[0].shape[0])] + [rows_of(ins[1:5])]
    outs[4][...] = ob[-1]
    put_window_parts(outs[:4], [dot(v.T, ins[5][...], 1, 0) for v in ob])


def middle_kernel(ins, outs):
    middle = total(ins[:5])
    normed, _ = norm_parts(middle)
    outs[0][...] = middle
    outs[1][...] = (normed * ins[5][...] + ins[6][...]).astype(BF16)


def middle_back_kernel(ins, outs):
    dh2 = ins[0][...] + ins[1][...].astype(F32)
    normed, inv = norm_parts(ins[2][...])
    back, g_scale, g_shift = norm_back(normed, inv, ins[4][...], dh2)
    dx2 = ins[3][...].astype(F32) + back
    outs[0][...] = dx2
    outs[1][...] = dx2.astype(BF16)
    outs[2][...] = jnp.concatenate([g_scale[None], g_shift[None]], axis=0)


def out_back_kernel(windows, ins, outs):
    for j, window in enumerate(windows):
        da = window_rows(ins[:4], window, outs[0].shape[2] // 4)
        outs[4][j] = da
        dob = dot(ins[4][...], da, 1, 1)
        for r in range(4):
            outs[r][j] = dob[r * HD : (r + 1) * HD].astype(BF16)


def merge_kernel(ins, outs):
    for j in range(outs[0].shape[0]):
        own, pair = ins[5 * j : 5 * j + 4], ins[5 * j + 4]
        for r in range(4):
            outs[r][j, :HD, :] = own[r][:HD, :]
            outs[r][j, HD:, :] = (own[r][HD:, :].astype(F32) + pair[r].astype(F32)).astype(BF16)


def project_back_kernel(ins, outs):
    w_in, cosine, sine = ins[4:7]
    c, s = cosine[...], sine[...]
    half = HD // 2
    pieces = []
    for r in range(4):
        for part in range(2):
            first = ins[r][part * HD : part * HD + half, :].astype(F32)
            second = ins[r][part * HD + half : (part + 1) * HD, :].astype(F32)
            pieces.append((first * c + second * s).astype(BF16))
            pieces.append((second * c - first * s).astype(BF16))
        pieces.append(ins[r][2 * HD :, :])
    d_proj = jnp.concatenate(pieces, axis=0)
    outs[0][...] = d_proj
    product = dot(d_proj.T, w_in[...], 1, 0)
    if len(outs) == 2:
        outs[1][...] = product.astype(BF16)
    else:
        put_window_parts(outs[1:], [r[...] for r in ins[7:]] + [product])


def input_back_kernel(ins, outs):
    dh1 = total(ins[:2])
    normed, inv = norm_parts(ins[2][...].astype(F32))
    back, _, _ = norm_back(normed, inv, ins[4][...], dh1)
    outs[0][...] = (ins[3][...] + back).astype(BF16)


def heads_kernel(ins, outs):
    back, w_in, gain, offset, slots, second = ins[:6]
    products, sums = 0.0, 0.0
    for d_proj, normed in zip(ins[6:9], ins[9:12]):
        products = products + dot(d_proj[...], normed[...], 1, 0)
        sums = sums + jnp.sum(d_proj[...].astype(F32), axis=1, keepdims=True)
    g_in = (products * gain[...] + sums * offset[...]).astype(BF16)
    wide = w_in[...].astype(F32)
    small = [
        jnp.sum(wide * products, axis=0, keepdims=True),
        second[:1, :],
        jnp.sum(wide * sums, axis=0, keepdims=True),
        second[1:, :],
    ]
    row = lax.broadcasted_iota(jnp.int32, (16, g_in.shape[1]), 0)
    small = [jnp.where(row == 0, v, 0.0).astype(BF16) for v in small]

    def put(out, slot, r):
        for chunk in range(4):
            if chunk < 3:
                rows = g_in[3 * HD * r + HD * chunk : 3 * HD * r + HD * (chunk + 1)]
            else:
                rows = back[HD * r : HD * (r + 1)].astype(BF16)
            out[slot, chunk, :HD] = rows
            out[slot, chunk, HD:] = small[chunk]

    for r in range(4):
        slot = slots[r]

        @pl.when(slot < 2)
        def _(slot=slot, r=r):
            put(outs[0], slot, r)

        @pl.when(slot >= 2)
        def _(slot=slot, r=r):
            put(outs[1], slot - 2, r)


def heads_core_kernel(ins, outs):
    for i in range(2):
        outs[i][...] = (ins[0][i].astype(F32) + ins[1][i].astype(F32)).astype(BF16)


def heads_pair_kernel(ins, outs):
    for r in range(4):
        chunk = lax.rem(ins[2][0] + r, 4)
        outs[r][...] = (ins[0][chunk].astype(F32) + ins[1][chunk].astype(F32)).astype(BF16)


def sum_kernel(ins, outs):
    outs[0][...] = total(ins).astype(outs[0].dtype)


def heads_ring_kernel(ins, outs):
    for r in range(4):
        chunk = lax.rem(ins[4][0] + r, 4)
        outs[0][chunk] = ins[r][...]
    for r in range(4):
        outs[1][lax.rem(ins[4][0] + r, 4)] = ins[r][HD : HD + 1].astype(F32)


def out_grad_kernel(ins, outs):
    outs[0][...] = sum(dot(ob[...], da[...], 1, 0) for ob, da in zip(ins[:3], ins[3:]))


def by_core(core, mine, other):
    low = jnp.where(core == 0, mine, other).astype(F32)
    high = jnp.where(core == 0, other, mine).astype(F32)
    return low, high


def units_final_kernel(ins, outs):
    low, high = by_core(ins[2][0], ins[0][...], ins[1][...])
    half = low.shape[0] // 3
    for side, values in enumerate((low, high)):
        for part in range(2):
            outs[0][part, :, side * half : (side + 1) * half] = values[
                part * half : (part + 1) * half
            ].T
        outs[1][side * half : (side + 1) * half] = values[2 * half :]


def heads_final_kernel(ins, outs):
    low, high = by_core(ins[2][0], ins[0][:, :HD], ins[1][:, :HD])
    for part in range(3):
        outs[0][part] = jnp.concatenate([low[part], high[part]], axis=0).T
    outs[1][...] = jnp.concatenate([low[3], high[3]], axis=0)


def halves_kernel(ins, outs):
    half = outs[0].shape[0]
    outs[0][...] = ins[0][:half]
    outs[1][...] = ins[1][half:]


def touch_kernel(ins, outs):
    outs[0][...] = jnp.zeros_like(outs[0])


def copy_kernel(ins, outs):
    for ref, out in zip(ins, outs):
        out[...] = ref[...]


def result_kernel(ins, outs):
    outs[0][...] = total(ins).astype(BF16)


def ffn_kernel(r, ins, outs):
    dy_in, own, recv, other, y = ins[-5:]
    dh2_out, y_out, hid_out, d_gu_out = outs[:4]
    h2 = rows_of(ins[:-5])
    dy = dy_in[lax.rem(y[0] + r, 4)]
    acc_dh2, acc_y = 0.0, 0.0
    for i, (w_gate, w_up, w_down) in enumerate(
        [[own[j, part] for part in range(3)] for j in range(2)]
        + [[ref[part] for part in range(3)] for ref in (recv, other)]
    ):
        gate = dot(h2, w_gate, 1, 1)
        up = dot(h2, w_up, 1, 1)
        dh = dot(dy, w_down, 1, 1)
        sig = 1.0 / (1.0 + jnp.exp(-gate))
        act = gate * sig
        hid = (act * up).astype(BF16)
        d_gate = (dh * up * (sig + act * (1.0 - sig))).astype(BF16)
        d_up = (dh * act).astype(BF16)
        hid_out[i] = hid
        d_gu_out[i, 0] = d_gate
        d_gu_out[i, 1] = d_up
        acc_dh2 = acc_dh2 + dot(d_gate, w_gate, 1, 0) + dot(d_up, w_up, 1, 0)
        acc_y = acc_y + dot(hid, w_down, 1, 0)
    dh2_out[...] = acc_dh2.astype(BF16)
    y_out[...] = acc_y.astype(BF16)


def ffn_grad_kernel(ins, outs):
    hid, d_gu, dy, flags = ins[:4], ins[4:8], ins[13], ins[14]
    h2_all = rows_of(ins[8:13])
    core, y = flags[0], flags[1]
    dy_all = jnp.concatenate([dy[lax.rem(y + r, 4)] for r in range(4)], axis=0)
    for out, slot, block in ((1, 0, 1 - core), (1, 1, 3), (0, 0, core), (0, 1, 2)):
        for part in range(2):
            d_block = jnp.concatenate([r[block, part] for r in d_gu], axis=0)
            outs[out][slot, part] = dot(d_block.T, h2_all, 1, 0).astype(BF16)
        hid_block = jnp.concatenate([r[block] for r in hid], axis=0)
        outs[out][slot, 2] = dot(hid_block.T, dy_all, 1, 0).astype(BF16)


def load_keys(own, pair, places):
    keys = jnp.concatenate([r[HD : 2 * HD, :] for r in own] + [pair[i, :HD] for i in range(4)], axis=1)
    values = jnp.concatenate([r[2 * HD :, :] for r in own] + [pair[i, HD:] for i in range(4)], axis=1)
    z, y, xl = places[0], places[1], places[2]
    tokens = own[0].shape[1]
    rows = tokens // 4
    lane = lax.broadcasted_iota(jnp.int32, (1, 8 * tokens), 1)
    source, within = lane // tokens, lane % tokens
    side = jnp.where(source < 4, xl, 1 - xl)
    at = ((z + 4 - source % 4) % 4) * (8 * rows) + ((y + within // rows) % 4) * (2 * rows)
    at = at + side * rows + within % rows
    bias = jnp.where(at < places[3], 0.0, MASKED)
    row = lax.broadcasted_iota(jnp.int32, (16, 8 * tokens), 0)
    extra = jnp.where(row == 0, bias, 0.0).astype(BF16)
    return keys, values, jnp.concatenate([keys, extra], axis=0)


def with_one(queries):
    row = lax.broadcasted_iota(jnp.int32, (16, queries.shape[1]), 0)
    return jnp.concatenate([queries, jnp.where(row == 0, 1.0, 0.0).astype(BF16)], axis=0)


def attend_kernel(ins, outs):
    own, pair, places, before = ins[0:4], ins[4], ins[5], ins[6:]
    out, wide, lse = outs[0:4], outs[4], outs[5]
    _, values, keys_bias = load_keys(own, pair, places)
    keys_rows = keys_bias.T
    for i in range(4):
        scores = dot(keys_rows, with_one(own[i][:HD, :]), 1, 0)
        top = jnp.max(scores, axis=0, keepdims=True)
        weights = jnp.exp(scores - top)
        total = jnp.sum(weights, axis=0, keepdims=True)
        attended = dot(values, weights.astype(BF16), 1, 0) * (1.0 / total)
        wide[i] = attended
        if before:
            out[i][0] = before[i][...]
            out[i][1] = attended.astype(BF16)
        else:
            out[i][...] = attended.astype(BF16)
        lse[i] = top + jnp.log(total)


def attend_back_kernel(ins, outs):
    own, pair, places = ins[0:4], ins[4], ins[5]
    dob, wide, lse = ins[6:10], ins[10], ins[11]
    d_own, d_pair = outs[0:4], outs[4]
    width = own[0].shape[1]
    keys, values, keys_bias = load_keys(own, pair, places)
    keys_rows = keys_bias.T
    values_rows = values.T
    dk = jnp.zeros((keys.shape[1], HD), F32)
    dv = jnp.zeros((keys.shape[1], HD), F32)
    for i in range(4):
        queries, grad = own[i][:HD, :], dob[i][...]
        scores = dot(keys_rows, with_one(queries), 1, 0)
        weights = jnp.exp(scores - lse[i])
        delta = jnp.sum(grad.astype(F32) * wide[i], axis=0, keepdims=True)
        grad_weights = dot(values_rows, grad, 1, 0)
        grad_scores = (weights * (grad_weights - delta)).astype(BF16)
        d_own[i][:HD, :] = (dot(keys, grad_scores, 1, 0) * 0.125).astype(BF16)
        dk = dk + dot(grad_scores, queries, 1, 1)
        dv = dv + dot(weights.astype(BF16), grad, 1, 1)
    dkv = jnp.concatenate([dk, dv], axis=1).T
    for i in range(4):
        d_own[i][HD:, :] = dkv[:, i * width : (i + 1) * width].astype(BF16)
        d_pair[i] = dkv[:, (4 + i) * width : (5 + i) * width].astype(BF16)


Y_GROUPS = [[0, 2, 4, 6], [1, 3, 5, 7]]


def shards(hidden_in, out_grad, norm_scales, norm_shifts, w_qkv, w_out, w_gate_up, w_down, lengths):
    rows, windows, width = hidden_in.shape
    tensor = lax.axis_index("tensor")
    y, xl = tensor // 2, tensor % 2
    z = lax.axis_index("blk")
    core = lax.axis_index("dp") % 2
    tokens = 4 * rows
    ff = w_down.shape[0]
    half = ff // 2

    order = []

    x_rows = hidden_in.transpose(1, 0, 2).reshape(windows * rows, width)
    dy_rows = out_grad.transpose(1, 0, 2).reshape(windows * rows, width)
    x_all = gather_y(x_rows)
    dy_abs = lax.all_gather(dy_rows, "tensor", axis=0, axis_index_groups=Y_GROUPS)

    y_index = jnp.full((1,), y, jnp.int32)
    z_index = jnp.full((1,), z, jnp.int32)
    flag = jnp.full((1,), core, jnp.int32)
    core_y = jnp.stack([core, y]).astype(jnp.int32)
    heads_at = (z + jnp.arange(4, dtype=jnp.int32)) % 4
    slots = jnp.where(heads_at // 2 == xl, 0, 1) + jnp.where(heads_at % 2 == core, 0, 2)
    places = jnp.where(heads_at // 2 == xl, heads_at % 2, 2 + ((heads_at % 2) ^ core))
    here = [jnp.stack([z, y, xl, lengths[w]]).astype(jnp.int32) for w in range(windows)]

    heads_own, heads_recv = call(
        heads_prepare_kernel, "heads_prepare", [w_qkv, w_out, flag],
        [((2, 4 * HD, width), BF16), ((4 * HD, width), BF16)], 0,
    )
    heads_recv = send_x(heads_recv, (-1, 1))
    units_own, units_recv = call(
        units_prepare_kernel, "units_prepare", [w_gate_up, w_down, flag],
        [((2, 3, half, width), BF16), ((3, half, width), BF16)], 0, [heads_own], 12,
    )
    w_in, w_back = call(
        heads_order_kernel, "heads_order", [heads_own, heads_recv, send_core(heads_recv), places],
        [((12 * HD, width), BF16), ((4 * HD, width), BF16)], 0, [units_own],
    )
    units_recv = send_x(units_recv, (-1, 1))
    units_other = send_core(units_recv)

    lane = jnp.arange(tokens, dtype=jnp.int32)
    within = ((y + lane // rows) % 4) * (2 * rows) + lane % rows
    inverse = 10000.0 ** (-(jnp.arange(HD // 2, dtype=F32) * 2.0) / HD)
    angles = inverse[:, None] * (z * (8 * rows) + within + xl * rows).astype(F32)[None, :]
    cosine, sine = jnp.cos(angles), jnp.sin(angles)

    gain = [norm_scales[i : i + 1] for i in range(2)]
    offset = [norm_shifts[i : i + 1] for i in range(2)]
    work = 2 * tokens * width * tokens
    piece, piece_wide = ((windows * rows, width), BF16), ((windows * rows, width), F32)
    head_piece, triple = ((HD, tokens), BF16), ((3 * HD, tokens), BF16)
    each = range(windows)

    def after(value):
        order.append(value)

    def last():
        return order[-1:]

    def add_core(kept, given, deps):
        shape = (kept.shape[1:], BF16)
        own, far = call(heads_core_kernel, "add_core", [kept, given], [shape] * 2, 0, deps)
        after(own)
        return own, far

    def run(kernel, name, inputs, outs, flops=0, mib=8, micros=4):
        out = call(kernel, name, inputs, outs, flops, last(), mib, micros)
        after(out[0])
        return out

    own, pair, wide, lse = ([None] * windows for _ in range(4))

    def entries(arrays, i):
        return [(v, i) for v in arrays]

    def project(*group):
        *sent, normed = run(
            functools.partial(project_kernel, group), "project",
            [*x_all, w_in, gain[0], offset[0], cosine, sine],
            [((len(group), 3 * HD, tokens), BF16)] * 4 + [((len(group), tokens, width), BF16)],
            3 * len(group) * work, 10,
        )
        sent = gather_z(sent)
        for i, w in enumerate(group):
            own[w] = entries(sent, i)
        return normed

    def stack(w):
        (pair[w],) = run(stack_kernel, "stack", own[w], [((4, 2 * HD, tokens), BF16)])
        pair[w] = send_pair(pair[w])

    def attend(w, before=()):
        *parts, wide[w], lse[w] = run(
            attend_kernel, "attend", [*own[w], pair[w], here[w], *before],
            [((2, HD, tokens) if before else (HD, tokens), BF16)] * 4
            + [((4, HD, tokens), F32), ((4, 1, tokens), F32)],
            128 * HD * tokens * tokens, 10,
        )
        return parts

    normed_all = [project(0), project(1, 2)]
    stack(0)
    stack(1)
    out = attend(0)
    stack(2)
    out = scatter_z(attend(1, out))
    out_last = scatter_z(attend(2))
    (ob,) = run(join_kernel, "join", out, [((2, 4 * HD, tokens), BF16)])
    *parts, ob_last = run(
        out_kernel, "out_project", [ob, *out_last, w_back],
        [piece] * 4 + [((4 * HD, tokens), BF16)], 3 * work,
    )
    middle, h2 = run(
        middle_kernel, "middle", [*scatter_y(parts), x_rows, gain[1], offset[1]], [piece_wide, piece]
    )

    h2_after, h2_before = send_y(h2, -1), send_y(h2, 1)
    run(touch_kernel, "touch", [dy_abs, units_own, units_recv, units_other], [((8, 128), F32)])
    near = run(halves_kernel, "halves", [h2_after, h2_before], [((windows * rows // 2, width), BF16)] * 2)
    h2_all = [h2, h2_after, [send_y(near[0], -1), send_y(near[1], 1)], h2_before]
    dh2, y_part, hid, d_gu = [None] * 4, [None] * 4, [None] * 4, [None] * 4
    for r in FFN_ORDER:
        dh2[r], y_part[r], hid[r], d_gu[r] = run(
            functools.partial(ffn_kernel, r), "ffn",
            [*(h2_all[r] if r == 2 else h2_all[r : r + 1]), dy_abs, units_own, units_recv, units_other, y_index],
            [piece, piece, ((4, windows * rows, half), BF16), ((4, 2, windows * rows, half), BF16)],
            18 * work, 10,
        )
        if r:
            dh2[r] = send_y(dh2[r], r)
    (dh2_near,) = run(sum_kernel, "add", [dh2[0], dh2[1], dh2[3]], [piece_wide])
    units, units_given = run(
        ffn_grad_kernel, "ffn_grad", [*hid, *d_gu, *h2_all[:2], *h2_all[2], h2_before, dy_abs, core_y],
        [((2, 3, half, width), BF16)] * 2, 36 * work, 10,
    )
    units_given = send_core(units_given)
    dx2, da, norm_sums = run(
        middle_back_kernel, "middle_back", [dh2_near, dh2[2], middle, dy_rows, gain[1]],
        [piece_wide, piece, ((2, width), F32)],
    )
    da_all = gather_y(da)

    def out_back(*group):
        *parts, rows_all = run(
            functools.partial(out_back_kernel, group), "out_back", [*da_all, w_back],
            [((len(group), HD, tokens), BF16)] * 4 + [((len(group), tokens, width), BF16)],
            len(group) * work, micros=20,
        )
        return gather_z(parts), rows_all

    def attend_back(w, dob):
        *d_own, d_pair = run(
            attend_back_kernel, "attend_back",
            [*own[w], pair[w], here[w], *dob, wide[w], lse[w]],
            [triple] * 4 + [((4, 2 * HD, tokens), BF16)], 320 * HD * tokens * tokens, 14,
        )
        return d_own, send_pair(d_pair)

    def merge(*parts):
        return scatter_z(
            run(
                merge_kernel, "merge", [v for d_own, d_pair in parts for v in (*d_own, d_pair)],
                [((len(parts), 3 * HD, tokens), BF16)] * 4,
            )
        )

    dob, da_rows = out_back(0)
    dob_rest, da_rest = out_back(1, 2)
    units, units_far = add_core(units, units_given, last())
    units_far = send_x(units_far, (-1, 1))
    d_first = attend_back(0, entries(dob, 0))
    d_second = attend_back(1, entries(dob_rest, 0))
    (units,) = run(sum_kernel, "add", [units, units_far], [(units.shape, BF16)])
    units = lax.psum_scatter(units.reshape(-1, width), "blk", scatter_dimension=0, tiled=True)
    def project_back(d_sent, earlier=(), last_one=False):
        return run(
            project_back_kernel, "project_back", [*entries(d_sent, 0), w_in, cosine, sine, *earlier],
            [((12 * HD, tokens), BF16)] + ([piece] * 4 if last_one else [((tokens, width), BF16)]),
            3 * work,
        )

    y_part = scatter_y(run(copy_kernel, "copy", y_part, [piece] * 4))
    d_first = merge(d_first)
    d_third = attend_back(2, entries(dob_rest, 1))
    d_second = merge(d_second)
    d_proj = [None] * windows
    d_proj[0], product_first = project_back(d_first)
    (g_back,) = run(
        out_grad_kernel, "out_grads", [(ob, 0), (ob, 1), ob_last, (da_rows, 0), (da_rest, 0), (da_rest, 1)],
        [((4 * HD, width), F32)], 3 * work,
    )
    d_third = merge(d_third)
    d_proj[1], product_second = project_back(d_second)
    (result,) = run(result_kernel, "result", [*y_part, middle], [piece])
    (units,) = run(sum_kernel, "add", [units, send_far(units)], [(units.shape, BF16)])
    units = lax.all_gather(units, "blk", axis=0, tiled=True)
    d_proj[2], *parts = project_back(d_third, [product_first, product_second], True)
    dh1 = scatter_y(parts)
    wide_heads = ((2, 4, HD + 16, width), BF16)
    heads, heads_given = run(
        heads_kernel, "heads",
        [g_back, w_in, gain[0], offset[0], slots, norm_sums, *d_proj]
        + [(normed_all[0], 0), (normed_all[1], 0), (normed_all[1], 1)],
        [wide_heads, wide_heads], 9 * work, 10,
    )
    heads, heads_far = add_core(heads, send_core(heads_given), last())
    heads_far = send_x(heads_far, (-1, 1))
    (dh1_near,) = run(sum_kernel, "add", [dh1[0], dh1[1], dh1[3]], [piece_wide])
    chunk = ((HD + 16, width), BF16)
    parts = run(heads_pair_kernel, "add_pair", [heads, heads_far, z_index], [chunk] * 4)
    parts = [parts[0]] + [send_z(parts[r], r) for r in (1, 2, 3)]
    (part,) = run(sum_kernel, "add", parts, [chunk])
    (part,) = run(sum_kernel, "add", [part, send_far(part)], [chunk])
    (grad_in,) = run(
        input_back_kernel, "input_back", [dh1_near, dh1[2], x_rows, dx2, gain[0]], [piece]
    )
    ring = [part] + [send_z(part, -r) for r in (1, 2, 3)]
    grad_gate_up, grad_down = run(
        units_final_kernel, "units_final", [units, send_core(units), flag],
        [((2, width, ff), F32), ((ff, width), F32)],
    )
    heads, small = run(
        heads_ring_kernel, "ring", [*ring, z_index],
        [((4, HD + 16, width), BF16), ((4, 1, width), F32)],
    )
    grad_qkv, grad_out = run(
        heads_final_kernel, "heads_final", [heads, send_core(heads), flag],
        [((3, width, 2 * HD), F32), ((2 * HD, width), F32)],
    )
    small = small.reshape(4, width)
    small = small + sum(send_y(small, r) for r in (1, 2, 3))

    return (
        result.reshape(windows, rows, width).transpose(1, 0, 2),
        grad_in.reshape(windows, rows, width).transpose(1, 0, 2),
        grad_qkv,
        grad_out,
        grad_gate_up,
        grad_down,
        small[:2],
        small[2:],
    )


def solution(mesh):
    placed = (
        P(("blk", "tensor"), "dp", None),
        P(("blk", "tensor"), "dp", None),
        P(),
        P(),
        P(None, None, "tensor"),
        P("tensor", None),
        P(None, None, "tensor"),
        P("tensor", None),
        P("dp"),
    )
    return jax.shard_map(
        shards,
        mesh=mesh,
        in_specs=placed,
        out_specs=(
            P(("blk", "tensor"), "dp", None),
            P(("blk", "tensor"), "dp", None),
            P(None, None, "tensor"),
            P("tensor", None),
            P(None, None, "tensor"),
            P("tensor", None),
            P(),
            P(),
        ),
        check_vma=False,
    )
```
